32 devices in a mesh: parts: 2 (over y), gx: 4 (over z), gy: 2 (over x), gz: 2 (over core).
Axes of the slice: x: 2, y: 2, z: 4, core: 2. Of those that a mesh axis runs over, the one named last changes fastest.
Arguments:
- adjoint_source: float32 [8, 256, 1024], P(('parts', 'gz'), 'gx', 'gy'), parts along dimension 0, may hold values from -8 to 8
- node_voltage: float32 [8, 256, 1024], P(('parts', 'gz'), 'gx', 'gy'), parts along dimension 0, may hold values from -6 to 6
- class_x: int32 [8, 256, 1024], P(('parts', 'gz'), 'gx', 'gy'), parts along dimension 0, may hold values from 0 to 7
- class_y: int32 [8, 256, 1024], P(('parts', 'gz'), 'gx', 'gy'), parts along dimension 0, may hold values from 0 to 7
- via_cond: float32 [8, 256, 1024], P(('parts', 'gz'), 'gx', 'gy'), parts along dimension 0, may hold values from 0.5 to 4
- layer_sheet: float32 [4], replicated, may hold values from 0.5 to 4
- width_table: float32 [8], replicated, may hold values from 0.5 to 2
Outputs:
- adjoint: float32 [8, 256, 1024], P(('parts', 'gz'), 'gx', 'gy'), parts along dimension 0
- grad_x: float32 [8, 256, 1024], P(('parts', 'gz'), 'gx', 'gy'), parts along dimension 0
- grad_y: float32 [8, 256, 1024], P(('parts', 'gz'), 'gx', 'gy'), parts along dimension 0
- grad_via: float32 [8, 256, 1024], P(('parts', 'gz'), 'gx', 'gy'), parts along dimension 0
The draws below stay inside these ranges and needn't reach their ends.
There are 2 independent parts, one for each index of `parts`. The reference program is written for one: setup_inputs(seed, part) draws one part's arguments, and reference() takes and returns one part's arrays. A program takes and returns all parts, laid end to end along the dimension named above; an argument that names none is the same for every part. Nothing has to cross between parts.
All inputs are finite; a program needn't handle non-finite values.
Results may differ from the reference program's by a relative error of at most 0.0001.
Values sent between devices are 32-bit elements; how exact they have to be, the bound alone decides.
A program may use at most 64 MiB of HBM per device.

```python
import math
import jax
import jax.numpy as jnp

ITERS = 2
NCLASS = 8
NX = 256
NY = 1024
LAYERS = 4


def draw_adjoint_source(key, part):
    key = jax.random.fold_in(key, 7)
    ramp = 0.6 + 1.4 * jnp.arange(NX, dtype=jnp.float32)[None, :, None] / NX
    rough = jnp.clip(jax.random.normal(key, (LAYERS, NX, NY), jnp.float32), -4.0, 4.0)
    return ramp * rough


def place_ends(array, rng, low, top_value):
    spot = [jax.random.randint(jax.random.fold_in(rng, axis), (), 0, length) for axis, length in enumerate(array.shape)]
    main_axis = array.shape.index(max(array.shape))
    neighbour = spot[:main_axis] + [(spot[main_axis] + 1) % array.shape[main_axis]] + spot[main_axis + 1:]
    return array.at[tuple(spot)].set(low).at[tuple(neighbour)].set(top_value)


def level_of(own_key, dims, cuts, low, high):
    def one(dim, parts):
        draws = jax.random.uniform(jax.random.fold_in(jax.random.fold_in(own_key, 6), dim), (parts,), jnp.float32, low / len(cuts), high / len(cuts))
        return jnp.repeat(jnp.exp(draws), dims[dim] // parts).reshape((-1,) + (1,) * (len(dims) - dim - 1))

    factor_of = one(*cuts[0])
    for cut in cuts[1:]:
        factor_of = factor_of * one(*cut)
    return factor_of


def gaussian(rng, extent, width, reach, pieces=(), held_as=jnp.bfloat16):
    values = jax.random.normal(rng, extent, jnp.float32) * width
    if len(pieces) > 0:
        values = level_of(rng, extent, pieces, -0.22, 0.18) * values
    return jnp.clip(values, min=-reach, max=reach).astype(held_as)


def setup_inputs(seed: int = 0, part: int = 0) -> dict:
    keys = jax.random.split(jax.random.key(seed), 8)
    own_keys = jax.random.split(jax.random.fold_in(keys[7], part), 8)
    return {
        "adjoint_source": draw_adjoint_source(jax.random.fold_in(jax.random.fold_in(keys[7], part), 71), part),
        "node_voltage": gaussian(own_keys[1], (LAYERS, NX, NY), 1.0, 6.0, ((0, 2), (1, 4), (2, 2)), jnp.float32),
        "class_x": place_ends(jax.random.randint(own_keys[2], (LAYERS, NX, NY), 0, NCLASS), jax.random.fold_in(own_keys[2], 1), 0, NCLASS - 1).astype(jnp.int32),
        "class_y": place_ends(jax.random.randint(own_keys[3], (LAYERS, NX, NY), 0, NCLASS), jax.random.fold_in(own_keys[3], 1), 0, NCLASS - 1).astype(jnp.int32),
        "via_cond": jnp.clip(jnp.exp(math.log(4.0) - 2.0794415 * jax.random.uniform(own_keys[4], (LAYERS, NX, NY), jnp.float32) ** level_of(own_keys[4], (LAYERS, NX, NY), ((0, 2), (1, 4), (2, 2)), -0.2, 0.2)), 0.5, 4.0),
        "layer_sheet": jnp.clip(jnp.exp(jax.random.uniform(keys[5], (LAYERS,), jnp.float32, math.log(0.5), math.log(4.0))), 0.5, 4.0),
        "width_table": jnp.clip(jnp.exp(jax.random.uniform(keys[6], (NCLASS,), jnp.float32, math.log(0.5), math.log(2.0))), 0.5, 2.0),
    }


def conductances(class_x, class_y, via_cond, layer_sheet, width_table):
    keep_x = (jnp.arange(NX) < NX - 1).astype(jnp.float32)[None, :, None]
    keep_y = (jnp.arange(NY) < NY - 1).astype(jnp.float32)[None, None, :]
    sheet = layer_sheet[:, None, None]
    cond_x = sheet * width_table[class_x] * keep_x
    cond_y = sheet * width_table[class_y] * keep_y
    return cond_x, cond_y, via_cond


def reference(adjoint_source, node_voltage, class_x, class_y, via_cond, layer_sheet, width_table):
    cond_x, cond_y, cond_v = conductances(class_x, class_y, via_cond, layer_sheet, width_table)
    lower_x = jnp.pad(cond_x, ((0, 0), (1, 0), (0, 0)))[:, :-1, :]
    lower_y = jnp.pad(cond_y, ((0, 0), (0, 0), (1, 0)))[:, :, :-1]
    lower_v = jnp.pad(cond_v, ((1, 0), (0, 0), (0, 0)))[:-1, :, :]
    diagonal = cond_x + lower_x + cond_y + lower_y + cond_v + lower_v

    def operate(field):
        padded = jnp.pad(field, 1)
        result = diagonal * field
        result = result - cond_x * padded[1:-1, 2:, 1:-1] - lower_x * padded[1:-1, :-2, 1:-1]
        result = result - cond_y * padded[1:-1, 1:-1, 2:] - lower_y * padded[1:-1, 1:-1, :-2]
        result = result - cond_v * padded[2:, 1:-1, 1:-1] - lower_v * padded[:-2, 1:-1, 1:-1]
        return result

    adjoint = jnp.zeros_like(adjoint_source)
    residual = adjoint_source
    precond = residual / diagonal
    direction = precond
    rho_now = jnp.sum(residual * precond)
    for iteration in range(ITERS):
        image = operate(direction)
        alpha = rho_now / jnp.sum(direction * image)
        adjoint = adjoint + alpha * direction
        residual = residual - alpha * image
        precond = residual / diagonal
        rho_next = jnp.sum(residual * precond)
        direction = precond + (rho_next / rho_now) * direction
        rho_now = rho_next

    pad_adj = jnp.pad(adjoint, 1)
    pad_volt = jnp.pad(node_voltage, 1)
    keep_x = (jnp.arange(NX) < NX - 1).astype(jnp.float32)[None, :, None]
    keep_y = (jnp.arange(NY) < NY - 1).astype(jnp.float32)[None, None, :]
    sheet = layer_sheet[:, None, None]
    grad_x = -sheet * keep_x * (adjoint - pad_adj[1:-1, 2:, 1:-1]) * (node_voltage - pad_volt[1:-1, 2:, 1:-1])
    grad_y = -sheet * keep_y * (adjoint - pad_adj[1:-1, 1:-1, 2:]) * (node_voltage - pad_volt[1:-1, 1:-1, 2:])
    grad_via = -(adjoint - pad_adj[2:, 1:-1, 1:-1]) * (node_voltage - pad_volt[2:, 1:-1, 1:-1])
    return adjoint, grad_x, grad_y, grad_via
```

```python
import functools

import jax
import jax.numpy as jnp
from jax import lax
from jax.experimental import pallas as pl
from jax.experimental.pallas import tpu as pltpu
from jax.sharding import PartitionSpec as P

F32 = jnp.float32
PAD = 8
ROWS = 16
LANES = 128
MESSAGES = {
    "cx": ("gx", 1), "cy": ("gy", 1), "cv": ("gz", 1),
    "vx": ("gx", -1), "vy": ("gy", -1), "vl": ("gz", -1),
    "zx_up": ("gx", 1), "zx_dn": ("gx", -1),
    "zy_up": ("gy", 1), "zy_dn": ("gy", -1),
    "zl_up": ("gz", 1), "zl_dn": ("gz", -1),
    "tx": ("gx", -1), "ty": ("gy", -1), "tl": ("gz", -1),
}
NAMES = list(MESSAGES)


def kernel(
    sizes, dims,
    source_hbm, volt_hbm, class_x_hbm, class_y_hbm, via_hbm, sheet_ref, table_ref,
    adj_ref, grad_x_ref, grad_y_ref, grad_v_ref,
    source, volt, class_x, class_y, via, cond_x, cond_y, low_y, inverse, z, t, adj,
    row_send, row_recv, col_send, col_recv, lay_recv, part, parts,
    load_sem, send_sem, recv_sem, part_send, part_recv,
):
    lay, nx, ny = dims
    group = sizes["gx"] * sizes["gy"] * sizes["gz"]
    here = {axis: lax.axis_index(axis) for axis in ("gx", "gy", "gz")}
    me = (here["gx"] * sizes["gy"] + here["gy"]) * sizes["gz"] + here["gz"]
    inner = pl.ds(PAD, nx)
    first, last = PAD, PAD + nx - 1

    loads = []
    for i, (src, dst) in enumerate((
        (class_x_hbm, class_x), (class_y_hbm, class_y), (via_hbm, via),
        (source_hbm, source), (volt_hbm, volt.at[:, inner, :]),
    )):
        copy = pltpu.make_async_copy(src, dst, load_sem.at[i])
        copy.start()
        loads.append(copy)

    row_recv[...] = jnp.zeros_like(row_recv)
    col_recv[...] = jnp.zeros_like(col_recv)
    lay_recv[...] = jnp.zeros_like(lay_recv)

    def place(rank):
        gz = lax.rem(rank, sizes["gz"])
        rest = lax.div(rank, sizes["gz"])
        return {"gx": lax.div(rest, sizes["gy"]), "gy": lax.rem(rest, sizes["gy"]), "gz": gz}

    barrier = pltpu.get_barrier_semaphore()

    def each_peer(body):
        if group <= 32:
            for k in range(1, group):
                body(lax.rem(me + k, group))
        else:
            lax.fori_loop(1, group, lambda k, c: (body(lax.rem(me + k, group)), c)[1], 0)

    each_peer(lambda peer: pl.semaphore_signal(
        barrier, inc=1, device_id=place(peer), device_id_type=pl.DeviceIdType.MESH))

    ROW = {"cx": 0, "vx": 1, "zx_up": 2, "zx_dn": 3, "tx": 4}
    COL = {"cy": 0, "vy": 1, "zy_up": 2, "zy_dn": 3, "ty": 4}
    LAY = {"cv": 0, "vl": 1, "zl_up": 2, "zl_dn": 3, "tl": 4}
    LAY_SRC = {
        "cv": via.at[lay - 1], "vl": volt.at[0, inner, :], "zl_up": z.at[lay - 1, inner, :],
        "zl_dn": z.at[0, inner, :], "tl": t.at[0, inner, :],
    }

    def message(name):
        axis, way = MESSAGES[name]
        i = NAMES.index(name)
        if name in ROW:
            src, dst = row_send.at[ROW[name]], row_recv.at[ROW[name]]
        elif name in COL:
            src, dst = col_send.at[COL[name]], col_recv.at[COL[name]]
        else:
            src, dst = LAY_SRC[name], lay_recv.at[LAY[name]]
        size = sizes[axis]
        to = lax.rem(here[axis] + (way + size), size)
        return pltpu.make_async_remote_copy(
            src_ref=src, dst_ref=dst, send_sem=send_sem.at[i], recv_sem=recv_sem.at[i],
            device_id={axis: to}, device_id_type=pl.DeviceIdType.MESH)

    def at_end(axis, way):
        return here[axis] == (sizes[axis] - 1 if way > 0 else 0)

    def send(*names):
        for name in names:
            axis, way = MESSAGES[name]
            if sizes[axis] > 1:
                pl.when(jnp.logical_not(at_end(axis, way)))(message(name).start)

    def receive(*names):
        for name in names:
            axis, way = MESSAGES[name]
            if sizes[axis] > 1:
                pl.when(jnp.logical_not(at_end(axis, -way)))(message(name).wait_recv)

    def sent(*names):
        for name in names:
            axis, way = MESSAGES[name]
            if sizes[axis] > 1:
                pl.when(jnp.logical_not(at_end(axis, way)))(message(name).wait_send)

    chunks = [(l, r) for l in range(lay) for r in range(0, nx, ROWS)]
    lane = lax.broadcasted_iota(jnp.int32, (ROWS, LANES), 1)

    def put_col(name, tile, at):
        col_send[COL[name]] = tile.reshape(lay * nx, LANES).T[at:at + 1, :]

    def col_halo(name):
        row = col_recv[COL[name]]
        return jnp.broadcast_to(row, (LANES, lay * nx)).T

    def from_left(value, edge):
        moved = pltpu.roll(value, 1, 1)
        head = jnp.where(lane == 0, edge, moved[:, :LANES])
        return jnp.concatenate([head, moved[:, LANES:]], axis=1)

    def from_right(value, edge):
        moved = pltpu.roll(value, ny - 1, 1)
        tail = jnp.where(lane == LANES - 1, edge, moved[:, ny - LANES:])
        return jnp.concatenate([moved[:, :ny - LANES], tail], axis=1)

    def edge_of(halo, l, r):
        return halo[l * nx + r:l * nx + r + ROWS]

    sheets = [sheet_ref[here["gz"] * lay + l] for l in range(lay)]
    classes = table_ref.shape[0]

    def look_up(label, l):
        value = jnp.full(label.shape, sheets[l] * table_ref[classes - 1], F32)
        for c in range(classes - 1):
            value = jnp.where(label == c, sheets[l] * table_ref[c], value)
        return value

    loads[0].wait()
    for l, r in chunks:
        cond_x[l, PAD + r:PAD + r + ROWS, :] = look_up(class_x[l, r:r + ROWS, :], l)

    @pl.when(at_end("gx", 1))
    def _():
        cond_x[:, last, :] = jnp.zeros((lay, ny), F32)

    loads[1].wait()
    for l, r in chunks:
        cond_y[l, r:r + ROWS, :] = look_up(class_y[l, r:r + ROWS, :], l)

    @pl.when(at_end("gy", 1))
    def _():
        for l in range(lay):
            tile = cond_y[l, :, ny - LANES:]
            spot = lax.broadcasted_iota(jnp.int32, tile.shape, 1)
            cond_y[l, :, ny - LANES:] = jnp.where(spot == LANES - 1, 0.0, tile)

    row_send[ROW["cx"]] = cond_x[:, last, :]
    put_col("cy", cond_y[:, :, ny - LANES:], LANES - 1)
    loads[2].wait()
    loads[3].wait()
    loads[4].wait()
    row_send[ROW["vx"]] = volt[:, first, :]
    put_col("vy", volt[:, inner, :LANES], 0)
    pl.semaphore_wait(barrier, group - 1)
    send("cv", "cx", "cy", "vx", "vy", "vl")
    receive("cx", "cy", "cv")

    cond_x[:, PAD - 1, :] = row_recv[ROW["cx"]]
    halo = col_halo("cy")
    moment0 = jnp.zeros((ROWS, ny), F32)
    for l, r in chunks:
        rows = slice(r, r + ROWS)
        cy = cond_y[l, rows, :]
        ly = from_left(cy, edge_of(halo, l, r))
        low_y[l, rows, :] = ly
        below = via[l - 1, rows, :] if l > 0 else lay_recv[LAY["cv"], rows, :]
        total = (cond_x[l, PAD + r:PAD + r + ROWS, :] + cond_x[l, PAD - 1 + r:PAD - 1 + r + ROWS, :]
                 + cy + ly + via[l, rows, :] + below)
        inv = 1.0 / total
        inverse[l, rows, :] = inv
        value = source[l, rows, :] * inv
        z[l, PAD + r:PAD + r + ROWS, :] = value
        moment0 = moment0 + source[l, rows, :] * value
    row_send[ROW["zx_up"]] = z[:, last, :]
    row_send[ROW["zx_dn"]] = z[:, first, :]
    put_col("zy_up", z[:, inner, ny - LANES:], LANES - 1)
    put_col("zy_dn", z[:, inner, :LANES], 0)
    send("zl_up", "zl_dn", "zx_up", "zx_dn", "zy_up", "zy_dn")

    receive("vx", "vy", "vl")
    volt[:, last + 1, :] = row_recv[ROW["vx"]]
    halo = col_halo("vy")
    for l, r in chunks:
        rows = slice(r, r + ROWS)
        v = volt[l, PAD + r:PAD + r + ROWS, :]
        above = volt[l + 1, PAD + r:PAD + r + ROWS, :] if l + 1 < lay else lay_recv[LAY["vl"], rows, :]
        grad_x_ref[l, rows, :] = -sheets[l] * (v - volt[l, PAD + 1 + r:PAD + 1 + r + ROWS, :])
        grad_y_ref[l, rows, :] = -sheets[l] * (v - from_right(v, edge_of(halo, l, r)))
        grad_v_ref[l, rows, :] = above - v

    @pl.when(at_end("gx", 1))
    def _():
        grad_x_ref[:, nx - 1, :] = jnp.zeros((lay, ny), F32)

    @pl.when(at_end("gy", 1))
    def _():
        for l in range(lay):
            tile = grad_y_ref[l, :, ny - LANES:]
            spot = lax.broadcasted_iota(jnp.int32, tile.shape, 1)
            grad_y_ref[l, :, ny - LANES:] = jnp.where(spot == LANES - 1, 0.0, tile)

    receive("zx_up", "zx_dn", "zy_up", "zy_dn", "zl_up", "zl_dn")
    z[:, PAD - 1, :] = row_recv[ROW["zx_up"]]
    z[:, last + 1, :] = row_recv[ROW["zx_dn"]]
    halo_lo = col_halo("zy_up")
    halo_hi = col_halo("zy_dn")
    moment1 = jnp.zeros((ROWS, ny), F32)
    moment2 = jnp.zeros((ROWS, ny), F32)
    for l, r in chunks:
        rows = slice(r, r + ROWS)
        mid = slice(PAD + r, PAD + r + ROWS)
        lower = slice(PAD - 1 + r, PAD - 1 + r + ROWS)
        upper = slice(PAD + 1 + r, PAD + 1 + r + ROWS)
        here_z = z[l, mid, :]
        z_above = z[l + 1, mid, :] if l + 1 < lay else lay_recv[LAY["zl_dn"], rows, :]
        z_below = z[l - 1, mid, :] if l > 0 else lay_recv[LAY["zl_up"], rows, :]
        below = via[l - 1, rows, :] if l > 0 else lay_recv[LAY["cv"], rows, :]
        s = cond_x[l, mid, :] * z[l, upper, :] + cond_x[l, lower, :] * z[l, lower, :]
        s = s + cond_y[l, rows, :] * from_right(here_z, edge_of(halo_hi, l, r))
        s = s + low_y[l, rows, :] * from_left(here_z, edge_of(halo_lo, l, r))
        s = s + via[l, rows, :] * z_above + below * z_below
        value = s * inverse[l, rows, :]
        t[l, mid, :] = value
        moment1 = moment1 + here_z * s
        moment2 = moment2 + value * s
    row_send[ROW["tx"]] = t[:, first, :]
    put_col("ty", t[:, inner, :LANES], 0)
    send("tl", "tx", "ty")
    receive("tx", "ty", "tl")
    t[:, last + 1, :] = row_recv[ROW["tx"]]
    halo_t = col_halo("ty")
    moment3 = jnp.zeros((ROWS, ny), F32)
    for l, r in chunks:
        rows = slice(r, r + ROWS)
        mid = slice(PAD + r, PAD + r + ROWS)
        upper = slice(PAD + 1 + r, PAD + 1 + r + ROWS)
        here_t = t[l, mid, :]
        t_above = t[l + 1, mid, :] if l + 1 < lay else lay_recv[LAY["tl"], rows, :]
        s = cond_x[l, mid, :] * t[l, upper, :]
        s = s + cond_y[l, rows, :] * from_right(here_t, edge_of(halo_t, l, r))
        s = s + via[l, rows, :] * t_above
        moment3 = moment3 + here_t * s

    def fold(value):
        wide = sum(value[:, k:k + LANES] for k in range(0, ny, LANES))
        return jnp.sum(wide, axis=0, keepdims=True)

    part[0:1, :] = fold(moment0)
    part[1:2, :] = fold(moment1)
    part[2:3, :] = fold(moment2)
    part[3:4, :] = 2.0 * fold(moment3)
    part[4:8, :] = jnp.zeros((4, LANES), F32)

    def share(peer, slot):
        return pltpu.make_async_remote_copy(
            src_ref=part, dst_ref=parts.at[slot], send_sem=part_send.at[peer], recv_sem=part_recv.at[slot],
            device_id=place(peer), device_id_type=pl.DeviceIdType.MESH)

    each_peer(lambda peer: share(peer, me).start())
    parts[me] = part[...]
    each_peer(lambda peer: share(peer, peer).wait_recv())
    totals = jnp.sum(jnp.sum(parts[...], axis=0), axis=1, keepdims=True)
    c0, c1, c2, c3 = (totals[k:k + 1, :] for k in range(4))
    curve = c0 - c1
    alpha = c0 / curve
    rest = -c1 / curve
    rho = rest * rest * c0 + 2.0 * rest * alpha * c1 + alpha * alpha * c2
    beta = rho / c0
    cross = rest * curve + alpha * (c1 - c2)
    own = rest * rest * curve + 2.0 * rest * alpha * (c1 - c2) + alpha * alpha * (c2 - c3)
    alpha_next = rho / (own + 2.0 * beta * cross + beta * beta * curve)
    factor_z = jnp.broadcast_to(alpha + alpha_next * (rest + beta), (1, ny))
    factor_t = jnp.broadcast_to(alpha_next * alpha, (1, ny))

    adj[:, last + 1, :] = factor_z * z[:, last + 1, :] + factor_t * t[:, last + 1, :]
    for l, r in chunks:
        mid = slice(PAD + r, PAD + r + ROWS)
        value = factor_z * z[l, mid, :] + factor_t * t[l, mid, :]
        adj[l, mid, :] = value
        adj_ref[l, r:r + ROWS, :] = value
    halo = factor_z[:, :LANES] * halo_hi + factor_t[:, :LANES] * halo_t
    for l, r in chunks:
        rows = slice(r, r + ROWS)
        mid = slice(PAD + r, PAD + r + ROWS)
        upper = slice(PAD + 1 + r, PAD + 1 + r + ROWS)
        value = adj[l, mid, :]
        if l + 1 < lay:
            above = adj[l + 1, mid, :]
        else:
            above = factor_z * lay_recv[LAY["zl_dn"], rows, :] + factor_t * lay_recv[LAY["tl"], rows, :]
        grad_x_ref[l, rows, :] = grad_x_ref[l, rows, :] * (value - adj[l, upper, :])
        grad_y_ref[l, rows, :] = grad_y_ref[l, rows, :] * (value - from_right(value, edge_of(halo, l, r)))
        grad_v_ref[l, rows, :] = grad_v_ref[l, rows, :] * (value - above)

    sent(*NAMES)
    each_peer(lambda peer: share(peer, me).wait_send())


def body(sizes, *args):
    lay, nx, ny = args[0].shape
    group = sizes["gx"] * sizes["gy"] * sizes["gz"]
    block = jax.ShapeDtypeStruct((lay, nx, ny), F32)
    whole = pl.BlockSpec(memory_space=pl.ANY)
    scalars = pl.BlockSpec(memory_space=pltpu.SMEM)
    vmem = pl.BlockSpec(memory_space=pltpu.VMEM)
    flat = lambda dtype=F32: pltpu.VMEM((lay, nx, ny), dtype)
    tall = pltpu.VMEM((lay, nx + 2 * PAD, ny), F32)
    return pl.pallas_call(
        functools.partial(kernel, sizes, (lay, nx, ny)),
        out_shape=(block,) * 4,
        in_specs=[whole] * 5 + [scalars] * 2,
        out_specs=(vmem,) * 4,
        scratch_shapes=[
            flat(), tall, flat(jnp.int32), flat(jnp.int32), flat(),
            tall, flat(), flat(), flat(), tall, tall, tall,
            pltpu.VMEM((5, lay, ny), F32), pltpu.VMEM((5, lay, ny), F32),
            pltpu.VMEM((5, 1, lay * nx), F32), pltpu.VMEM((5, 1, lay * nx), F32),
            pltpu.VMEM((5, nx, ny), F32),
            pltpu.VMEM((8, LANES), F32), pltpu.VMEM((group, 8, LANES), F32),
            pltpu.SemaphoreType.DMA((5,)),
            pltpu.SemaphoreType.DMA((len(NAMES),)), pltpu.SemaphoreType.DMA((len(NAMES),)),
            pltpu.SemaphoreType.DMA((group,)), pltpu.SemaphoreType.DMA((group,)),
        ],
        compiler_params=pltpu.CompilerParams(
            collective_id=0, has_side_effects=True, vmem_limit_bytes=32 * 1024 * 1024),
    )(*args)


def solution(mesh):
    placed = P(("parts", "gz"), "gx", "gy")
    sizes = {axis: mesh.shape[axis] for axis in ("gx", "gy", "gz")}
    return jax.shard_map(
        functools.partial(body, sizes),
        mesh=mesh,
        in_specs=(placed,) * 5 + (P(), P()),
        out_specs=(placed,) * 4,
        check_vma=False,
    )
```

```python
import functools

import jax
import jax.numpy as jnp
from jax import lax
from jax.experimental import pallas as pl
from jax.experimental.pallas import tpu as pltpu
from jax.sharding import PartitionSpec as P

F32 = jnp.float32
PAD = 8
ROWS = 16
LANES = 128
MESSAGES = {
    "cx": ("gx", 1), "cy": ("gy", 1), "cv": ("gz", 1),
    "vx": ("gx", -1), "vy": ("gy", -1), "vl": ("gz", -1),
    "zx_up": ("gx", 1), "zx_dn": ("gx", -1),
    "zy_up": ("gy", 1), "zy_dn": ("gy", -1),
    "zl_up": ("gz", 1), "zl_dn": ("gz", -1),
    "tx": ("gx", -1), "ty": ("gy", -1), "tl": ("gz", -1),
}
NAMES = list(MESSAGES)


def kernel(
    sizes, dims,
    source_hbm, volt_hbm, class_x_hbm, class_y_hbm, via_hbm, sheet_ref, table_ref,
    adj_ref, grad_x_ref, grad_y_ref, grad_v_ref,
    source, volt, class_x, class_y, via, cond_x, cond_y, low_y, inverse, z, t, adj,
    row_send, row_recv, col_send, col_recv, lay_recv, part, parts,
    load_sem, send_sem, recv_sem, part_send, part_recv,
):
    lay, nx, ny = dims
    group = sizes["gx"] * sizes["gy"] * sizes["gz"]
    here = {axis: lax.axis_index(axis) for axis in ("gx", "gy", "gz")}
    me = (here["gx"] * sizes["gy"] + here["gy"]) * sizes["gz"] + here["gz"]
    inner = pl.ds(PAD, nx)
    first, last = PAD, PAD + nx - 1

    loads = []
    for i, (src, dst) in enumerate((
        (class_x_hbm, class_x), (class_y_hbm, class_y), (via_hbm, via),
        (source_hbm, source), (volt_hbm, volt.at[:, inner, :]),
    )):
        copy = pltpu.make_async_copy(src, dst, load_sem.at[i])
        copy.start()
        loads.append(copy)

    row_recv[...] = jnp.zeros_like(row_recv)
    col_recv[...] = jnp.zeros_like(col_recv)
    lay_recv[...] = jnp.zeros_like(lay_recv)

    def place(rank):
        gz = lax.rem(rank, sizes["gz"])
        rest = lax.div(rank, sizes["gz"])
        return {"gx": lax.div(rest, sizes["gy"]), "gy": lax.rem(rest, sizes["gy"]), "gz": gz}

    barrier = pltpu.get_barrier_semaphore()

    def each_peer(body):
        if group <= 32:
            for k in range(1, group):
                body(lax.rem(me + k, group))
        else:
            lax.fori_loop(1, group, lambda k, c: (body(lax.rem(me + k, group)), c)[1], 0)

    each_peer(lambda peer: pl.semaphore_signal(
        barrier, inc=1, device_id=place(peer), device_id_type=pl.DeviceIdType.MESH))

    ROW = {"cx": 0, "vx": 1, "zx_up": 2, "zx_dn": 3, "tx": 4}
    COL = {"cy": 0, "vy": 1, "zy_up": 2, "zy_dn": 3, "ty": 4}
    LAY = {"cv": 0, "vl": 1, "zl_up": 2, "zl_dn": 3, "tl": 4}
    LAY_SRC = {
        "cv": via.at[lay - 1], "vl": volt.at[0, inner, :], "zl_up": z.at[lay - 1, inner, :],
        "zl_dn": z.at[0, inner, :], "tl": t.at[0, inner, :],
    }

    def message(name):
        axis, way = MESSAGES[name]
        i = NAMES.index(name)
        if name in ROW:
            src, dst = row_send.at[ROW[name]], row_recv.at[ROW[name]]
        elif name in COL:
            src, dst = col_send.at[COL[name]], col_recv.at[COL[name]]
        else:
            src, dst = LAY_SRC[name], lay_recv.at[LAY[name]]
        size = sizes[axis]
        to = lax.rem(here[axis] + (way + size), size)
        return pltpu.make_async_remote_copy(
            src_ref=src, dst_ref=dst, send_sem=send_sem.at[i], recv_sem=recv_sem.at[i],
            device_id={axis: to}, device_id_type=pl.DeviceIdType.MESH)

    def at_end(axis, way):
        return here[axis] == (sizes[axis] - 1 if way > 0 else 0)

    def send(*names):
        for name in names:
            axis, way = MESSAGES[name]
            if sizes[axis] > 1:
                pl.when(jnp.logical_not(at_end(axis, way)))(message(name).start)

    def receive(*names):
        for name in names:
            axis, way = MESSAGES[name]
            if sizes[axis] > 1:
                pl.when(jnp.logical_not(at_end(axis, -way)))(message(name).wait_recv)

    def sent(*names):
        for name in names:
            axis, way = MESSAGES[name]
            if sizes[axis] > 1:
                pl.when(jnp.logical_not(at_end(axis, way)))(message(name).wait_send)

    chunks = [(l, r) for l in range(lay) for r in range(0, nx, ROWS)]
    lane = lax.broadcasted_iota(jnp.int32, (ROWS, LANES), 1)

    def put_col(name, tile, at):
        col_send[COL[name]] = tile.reshape(lay * nx, LANES).T[at:at + 1, :]

    def col_halo(name):
        row = col_recv[COL[name]]
        return jnp.broadcast_to(row, (LANES, lay * nx)).T

    def from_left(value, edge):
        moved = pltpu.roll(value, 1, 1)
        head = jnp.where(lane == 0, edge, moved[:, :LANES])
        return jnp.concatenate([head, moved[:, LANES:]], axis=1)

    def from_right(value, edge):
        moved = pltpu.roll(value, ny - 1, 1)
        tail = jnp.where(lane == LANES - 1, edge, moved[:, ny - LANES:])
        return jnp.concatenate([moved[:, :ny - LANES], tail], axis=1)

    def edge_of(halo, l, r):
        return halo[l * nx + r:l * nx + r + ROWS]

    sheets = [sheet_ref[here["gz"] * lay + l] for l in range(lay)]
    classes = table_ref.shape[0]

    def look_up(label, l):
        value = jnp.full(label.shape, sheets[l] * table_ref[classes - 1], F32)
        for c in range(classes - 1):
            value = jnp.where(label == c, sheets[l] * table_ref[c], value)
        return value

    loads[0].wait()
    for l, r in chunks:
        cond_x[l, PAD + r:PAD + r + ROWS, :] = look_up(class_x[l, r:r + ROWS, :], l)

    @pl.when(at_end("gx", 1))
    def _():
        cond_x[:, last, :] = jnp.zeros((lay, ny), F32)

    loads[1].wait()
    for l, r in chunks:
        cond_y[l, r:r + ROWS, :] = look_up(class_y[l, r:r + ROWS, :], l)

    @pl.when(at_end("gy", 1))
    def _():
        for l in range(lay):
            tile = cond_y[l, :, ny - LANES:]
            spot = lax.broadcasted_iota(jnp.int32, tile.shape, 1)
            cond_y[l, :, ny - LANES:] = jnp.where(spot == LANES - 1, 0.0, tile)

    row_send[ROW["cx"]] = cond_x[:, last, :]
    put_col("cy", cond_y[:, :, ny - LANES:], LANES - 1)
    loads[2].wait()
    loads[3].wait()
    loads[4].wait()
    row_send[ROW["vx"]] = volt[:, first, :]
    put_col("vy", volt[:, inner, :LANES], 0)
    pl.semaphore_wait(barrier, group - 1)
    send("cv", "cx", "cy", "vx", "vy", "vl")
    receive("cx", "cy", "cv")

    cond_x[:, PAD - 1, :] = row_recv[ROW["cx"]]
    halo = col_halo("cy")
    moment0 = jnp.zeros((ROWS, ny), F32)
    for l, r in chunks:
        rows = slice(r, r + ROWS)
        cy = cond_y[l, rows, :]
        ly = from_left(cy, edge_of(halo, l, r))
        low_y[l, rows, :] = ly
        below = via[l - 1, rows, :] if l > 0 else lay_recv[LAY["cv"], rows, :]
        total = (cond_x[l, PAD + r:PAD + r + ROWS, :] + cond_x[l, PAD - 1 + r:PAD - 1 + r + ROWS, :]
                 + cy + ly + via[l, rows, :] + below)
        inv = 1.0 / total
        inverse[l, rows, :] = inv
        value = source[l, rows, :] * inv
        z[l, PAD + r:PAD + r + ROWS, :] = value
        moment0 = moment0 + source[l, rows, :] * value
    row_send[ROW["zx_up"]] = z[:, last, :]
    row_send[ROW["zx_dn"]] = z[:, first, :]
    put_col("zy_up", z[:, inner, ny - LANES:], LANES - 1)
    put_col("zy_dn", z[:, inner, :LANES], 0)
    send("zl_up", "zl_dn", "zx_up", "zx_dn", "zy_up", "zy_dn")

    receive("vx", "vy", "vl")
    volt[:, last + 1, :] = row_recv[ROW["vx"]]
    halo = col_halo("vy")
    for l, r in chunks:
        rows = slice(r, r + ROWS)
        v = volt[l, PAD + r:PAD + r + ROWS, :]
        above = volt[l + 1, PAD + r:PAD + r + ROWS, :] if l + 1 < lay else lay_recv[LAY["vl"], rows, :]
        grad_x_ref[l, rows, :] = -sheets[l] * (v - volt[l, PAD + 1 + r:PAD + 1 + r + ROWS, :])
        grad_y_ref[l, rows, :] = -sheets[l] * (v - from_right(v, edge_of(halo, l, r)))
        grad_v_ref[l, rows, :] = above - v

    @pl.when(at_end("gx", 1))
    def _():
        grad_x_ref[:, nx - 1, :] = jnp.zeros((lay, ny), F32)

    @pl.when(at_end("gy", 1))
    def _():
        for l in range(lay):
            tile = grad_y_ref[l, :, ny - LANES:]
            spot = lax.broadcasted_iota(jnp.int32, tile.shape, 1)
            grad_y_ref[l, :, ny - LANES:] = jnp.where(spot == LANES - 1, 0.0, tile)

    receive("zx_up", "zx_dn", "zy_up", "zy_dn", "zl_up", "zl_dn")
    z[:, PAD - 1, :] = row_recv[ROW["zx_up"]]
    z[:, last + 1, :] = row_recv[ROW["zx_dn"]]
    halo_lo = col_halo("zy_up")
    halo_hi = col_halo("zy_dn")
    moment1 = jnp.zeros((ROWS, ny), F32)
    moment2 = jnp.zeros((ROWS, ny), F32)
    for l, r in chunks:
        rows = slice(r, r + ROWS)
        mid = slice(PAD + r, PAD + r + ROWS)
        lower = slice(PAD - 1 + r, PAD - 1 + r + ROWS)
        upper = slice(PAD + 1 + r, PAD + 1 + r + ROWS)
        here_z = z[l, mid, :]
        z_above = z[l + 1, mid, :] if l + 1 < lay else lay_recv[LAY["zl_dn"], rows, :]
        z_below = z[l - 1, mid, :] if l > 0 else lay_recv[LAY["zl_up"], rows, :]
        below = via[l - 1, rows, :] if l > 0 else lay_recv[LAY["cv"], rows, :]
        s = cond_x[l, mid, :] * z[l, upper, :] + cond_x[l, lower, :] * z[l, lower, :]
        s = s + cond_y[l, rows, :] * from_right(here_z, edge_of(halo_hi, l, r))
        s = s + low_y[l, rows, :] * from_left(here_z, edge_of(halo_lo, l, r))
        s = s + via[l, rows, :] * z_above + below * z_below
        value = s * inverse[l, rows, :]
        t[l, mid, :] = value
        moment1 = moment1 + here_z * s
        moment2 = moment2 + value * s
    row_send[ROW["tx"]] = t[:, first, :]
    put_col("ty", t[:, inner, :LANES], 0)
    send("tl", "tx", "ty")
    receive("tx", "ty", "tl")
    t[:, last + 1, :] = row_recv[ROW["tx"]]
    halo_t = col_halo("ty")
    moment3 = jnp.zeros((ROWS, ny), F32)
    for l, r in chunks:
        rows = slice(r, r + ROWS)
        mid = slice(PAD + r, PAD + r + ROWS)
        upper = slice(PAD + 1 + r, PAD + 1 + r + ROWS)
        here_t = t[l, mid, :]
        t_above = t[l + 1, mid, :] if l + 1 < lay else lay_recv[LAY["tl"], rows, :]
        s = cond_x[l, mid, :] * t[l, upper, :]
        s = s + cond_y[l, rows, :] * from_right(here_t, edge_of(halo_t, l, r))
        s = s + via[l, rows, :] * t_above
        moment3 = moment3 + here_t * s

    def fold(value):
        wide = sum(value[:, k:k + LANES] for k in range(0, ny, LANES))
        return jnp.sum(wide, axis=0, keepdims=True)

    part[0:1, :] = fold(moment0)
    part[1:2, :] = fold(moment1)
    part[2:3, :] = fold(moment2)
    part[3:4, :] = 2.0 * fold(moment3)
    part[4:8, :] = jnp.zeros((4, LANES), F32)

    def share(peer, slot):
        return pltpu.make_async_remote_copy(
            src_ref=part, dst_ref=parts.at[slot], send_sem=part_send.at[peer], recv_sem=part_recv.at[slot],
            device_id=place(peer), device_id_type=pl.DeviceIdType.MESH)

    each_peer(lambda peer: share(peer, me).start())
    parts[me] = part[...]
    each_peer(lambda peer: share(peer, peer).wait_recv())
    totals = jnp.sum(jnp.sum(parts[...], axis=0), axis=1, keepdims=True)
    c0, c1, c2, c3 = (totals[k:k + 1, :] for k in range(4))
    curve = c0 - c1
    alpha = c0 / curve
    rest = -c1 / curve
    rho = rest * rest * c0 + 2.0 * rest * alpha * c1 + alpha * alpha * c2
    beta = rho / c0
    cross = rest * curve + alpha * (c1 - c2)
    own = rest * rest * curve + 2.0 * rest * alpha * (c1 - c2) + alpha * alpha * (c2 - c3)
    alpha_next = rho / (own + 2.0 * beta * cross + beta * beta * curve)
    factor_z = jnp.broadcast_to(alpha + alpha_next * (rest + beta), (1, ny))
    factor_t = jnp.broadcast_to(alpha_next * alpha, (1, ny))

    adj[:, last + 1, :] = factor_z * z[:, last + 1, :] + factor_t * t[:, last + 1, :]
    for l, r in chunks:
        mid = slice(PAD + r, PAD + r + ROWS)
        value = factor_z * z[l, mid, :] + factor_t * t[l, mid, :]
        adj[l, mid, :] = value
        adj_ref[l, r:r + ROWS, :] = value
    halo = factor_z[:, :LANES] * halo_hi + factor_t[:, :LANES] * halo_t
    for l, r in chunks:
        rows = slice(r, r + ROWS)
        mid = slice(PAD + r, PAD + r + ROWS)
        upper = slice(PAD + 1 + r, PAD + 1 + r + ROWS)
        value = adj[l, mid, :]
        if l + 1 < lay:
            above = adj[l + 1, mid, :]
        else:
            above = factor_z * lay_recv[LAY["zl_dn"], rows, :] + factor_t * lay_recv[LAY["tl"], rows, :]
        grad_x_ref[l, rows, :] = grad_x_ref[l, rows, :] * (value - adj[l, upper, :])
        grad_y_ref[l, rows, :] = grad_y_ref[l, rows, :] * (value - from_right(value, edge_of(halo, l, r)))
        grad_v_ref[l, rows, :] = grad_v_ref[l, rows, :] * (value - above)

    sent(*NAMES)
    each_peer(lambda peer: share(peer, me).wait_send())


def write_out(*refs):
    sem = refs[-1]
    copies = [pltpu.make_async_copy(refs[i], refs[4 + i], sem.at[i]) for i in range(4)]
    for copy in copies:
        copy.start()
    for copy in copies:
        copy.wait()


def body(sizes, *args):
    lay, nx, ny = args[0].shape
    group = sizes["gx"] * sizes["gy"] * sizes["gz"]
    block = jax.ShapeDtypeStruct((lay, nx, ny), F32)
    whole = pl.BlockSpec(memory_space=pltpu.HBM)
    scalars = pl.BlockSpec(memory_space=pltpu.SMEM)
    vmem = pl.BlockSpec(memory_space=pltpu.VMEM)
    flat = lambda dtype=F32: pltpu.VMEM((lay, nx, ny), dtype)
    tall = pltpu.VMEM((lay, nx + 2 * PAD, ny), F32)
    args = [pltpu.with_memory_space_constraint(a, pltpu.HBM) for a in args]
    results = pl.pallas_call(
        functools.partial(kernel, sizes, (lay, nx, ny)),
        out_shape=(block,) * 4,
        in_specs=[whole] * 5 + [scalars] * 2,
        out_specs=(vmem,) * 4,
        scratch_shapes=[
            flat(), tall, flat(jnp.int32), flat(jnp.int32), flat(),
            tall, flat(), flat(), flat(), tall, tall, tall,
            pltpu.VMEM((5, lay, ny), F32), pltpu.VMEM((5, lay, ny), F32),
            pltpu.VMEM((5, 1, lay * nx), F32), pltpu.VMEM((5, 1, lay * nx), F32),
            pltpu.VMEM((5, nx, ny), F32),
            pltpu.VMEM((8, LANES), F32), pltpu.VMEM((group, 8, LANES), F32),
            pltpu.SemaphoreType.DMA((5,)),
            pltpu.SemaphoreType.DMA((len(NAMES),)), pltpu.SemaphoreType.DMA((len(NAMES),)),
            pltpu.SemaphoreType.DMA((group,)), pltpu.SemaphoreType.DMA((group,)),
        ],
        compiler_params=pltpu.CompilerParams(
            collective_id=0, has_side_effects=True, vmem_limit_bytes=32 * 1024 * 1024),
    )(*args)
    return pl.pallas_call(
        write_out,
        out_shape=(block,) * 4,
        in_specs=[pl.BlockSpec(memory_space=pl.ANY)] * 4, compiler_params=pltpu.CompilerParams(vmem_limit_bytes=1024*1024),
        out_specs=(whole,) * 4,
        scratch_shapes=[pltpu.SemaphoreType.DMA((4,))],
    )(*results)


def solution(mesh):
    placed = P(("parts", "gz"), "gx", "gy")
    sizes = {axis: mesh.shape[axis] for axis in ("gx", "gy", "gz")}
    return jax.shard_map(
        functools.partial(body, sizes),
        mesh=mesh,
        in_specs=(placed,) * 5 + (P(), P()),
        out_specs=(placed,) * 4,
        check_vma=False,
    )
```

```python
import functools

import jax
import jax.numpy as jnp
from jax import lax
from jax.experimental import pallas as pl
from jax.experimental.pallas import tpu as pltpu
from jax.sharding import PartitionSpec as P

F32 = jnp.float32
PAD = 8
ROWS = 16
LANES = 128
MESSAGES = {
    "cx": {"gx": 1}, "cy": {"gy": 1}, "cv": {"gz": 1},
    "vx": {"gx": -1}, "vy": {"gy": -1}, "vl": {"gz": -1},
    "zx_up": {"gx": 1}, "zy_up": {"gy": 1}, "zl_up": {"gz": 1}, "zl_dn": {"gz": -1},
    "xd": {"gx": -1}, "yd": {"gy": -1}, "tl": {"gz": -1},
    "lx_up": {"gx": -1, "gz": 1}, "lx_dn": {"gx": -1, "gz": -1},
    "ly_up": {"gy": -1, "gz": 1}, "ly_dn": {"gy": -1, "gz": -1},
    "ca": {"gx": -1, "gy": 1}, "cb": {"gx": -1, "gy": -1}, "cc": {"gx": -1, "gy": -1},
    "cd": {"gx": 1, "gy": -1},
}
NAMES = list(MESSAGES)


def kernel(
    sizes, dims,
    source_hbm, volt_hbm, class_x_hbm, class_y_hbm, via_hbm, sheet_ref, table_ref,
    adj_ref, grad_x_ref, grad_y_ref, grad_v_ref,
    source, volt, class_x, class_y, via, cond_x, cond_y, low_y, inverse, z, t, adj,
    row_send, row_recv, col_send, col_recv, lay_recv,
    xd_send, xd_recv, yd_send, yd_recv, over_send, over_recv, row_end_send, row_end_recv,
    col_end_send, col_end_recv, part, parts,
    load_sem, send_sem, recv_sem, part_send, part_recv,
):
    lay, nx, ny = dims
    group = sizes["gx"] * sizes["gy"] * sizes["gz"]
    here = {axis: lax.axis_index(axis) for axis in ("gx", "gy", "gz")}
    me = (here["gx"] * sizes["gy"] + here["gy"]) * sizes["gz"] + here["gz"]
    inner = pl.ds(PAD, nx)
    first, last = PAD, PAD + nx - 1

    loads = []
    for i, (src, dst) in enumerate((
        (class_x_hbm, class_x), (class_y_hbm, class_y), (via_hbm, via),
        (source_hbm, source), (volt_hbm, volt.at[:, inner, :]),
    )):
        copy = pltpu.make_async_copy(src, dst, load_sem.at[i])
        copy.start()
        loads.append(copy)

    row_recv[...] = jnp.zeros_like(row_recv)
    col_recv[...] = jnp.zeros_like(col_recv)
    lay_recv[...] = jnp.zeros_like(lay_recv)
    for ref in (xd_recv, yd_recv, over_recv, row_end_recv, col_end_recv):
        ref[...] = jnp.zeros_like(ref)
    z[:, PAD - 1, :] = jnp.zeros((lay, ny), F32)
    z[:, last + 1, :] = jnp.zeros((lay, ny), F32)

    def place(rank):
        gz = lax.rem(rank, sizes["gz"])
        rest = lax.div(rank, sizes["gz"])
        return {"gx": lax.div(rest, sizes["gy"]), "gy": lax.rem(rest, sizes["gy"]), "gz": gz}

    barrier = pltpu.get_barrier_semaphore()

    def each_peer(body):
        if group <= 32:
            for k in range(1, group):
                body(lax.rem(me + k, group))
        else:
            lax.fori_loop(1, group, lambda k, c: (body(lax.rem(me + k, group)), c)[1], 0)

    each_peer(lambda peer: pl.semaphore_signal(
        barrier, inc=1, device_id=place(peer), device_id_type=pl.DeviceIdType.MESH))

    ROW = {"cx": 0, "vx": 1, "zx_up": 2}
    COL = {"cy": 0, "vy": 1, "zy_up": 2, "ly_up": 3, "ly_dn": 4}
    LAY = {"cv": 0, "vl": 1, "zl_up": 2, "zl_dn": 3, "tl": 4}
    LAY_SRC = {
        "cv": via.at[lay - 1], "vl": volt.at[0, inner, :], "zl_up": z.at[lay - 1, inner, :],
        "zl_dn": z.at[0, inner, :], "tl": t.at[0, inner, :],
    }

    OTHER = {
        "xd": (xd_send, xd_recv), "yd": (yd_send, yd_recv),
        "lx_up": (over_send.at[0], over_recv.at[0]), "lx_dn": (over_send.at[1], over_recv.at[1]),
        "ca": (row_end_send.at[0], row_end_recv.at[0]), "cb": (row_end_send.at[1], row_end_recv.at[1]),
        "cc": (col_end_send.at[0], col_end_recv.at[0]), "cd": (col_end_send.at[1], col_end_recv.at[1]),
    }

    def message(name):
        i = NAMES.index(name)
        if name in ROW:
            src, dst = row_send.at[ROW[name]], row_recv.at[ROW[name]]
        elif name in COL:
            src, dst = col_send.at[COL[name]], col_recv.at[COL[name]]
        elif name in OTHER:
            src, dst = OTHER[name]
        else:
            src, dst = LAY_SRC[name], lay_recv.at[LAY[name]]
        to = {axis: lax.rem(here[axis] + (way + sizes[axis]), sizes[axis])
              for axis, way in MESSAGES[name].items()}
        return pltpu.make_async_remote_copy(
            src_ref=src, dst_ref=dst, send_sem=send_sem.at[i], recv_sem=recv_sem.at[i],
            device_id=to, device_id_type=pl.DeviceIdType.MESH)

    def at_end(axis, way):
        return here[axis] == (sizes[axis] - 1 if way > 0 else 0)

    def guarded(name, sign, action):
        ways = MESSAGES[name]
        if any(sizes[axis] == 1 for axis in ways):
            return
        inside = [jnp.logical_not(at_end(axis, sign * way)) for axis, way in ways.items()]
        pl.when(functools.reduce(jnp.logical_and, inside))(action)

    def send(*names):
        for name in names:
            guarded(name, 1, message(name).start)

    def receive(*names):
        for name in names:
            guarded(name, -1, message(name).wait_recv)

    def sent(*names):
        for name in names:
            guarded(name, 1, message(name).wait_send)

    chunks = [(l, r) for l in range(lay) for r in range(0, nx, ROWS)]
    lane = lax.broadcasted_iota(jnp.int32, (ROWS, LANES), 1)

    def as_row(tile, at):
        return tile.reshape(lay * nx, LANES).T[at:at + 1, :]

    def put_col(name, tile, at):
        col_send[COL[name]] = as_row(tile, at)

    def as_col(row):
        return jnp.broadcast_to(row, (LANES, lay * nx)).T

    def col_halo(name):
        return as_col(col_recv[COL[name]])

    def from_left(value, edge):
        moved = pltpu.roll(value, 1, 1)
        head = jnp.where(lane == 0, edge, moved[:, :LANES])
        return jnp.concatenate([head, moved[:, LANES:]], axis=1)

    def from_right(value, edge):
        moved = pltpu.roll(value, ny - 1, 1)
        tail = jnp.where(lane == LANES - 1, edge, moved[:, ny - LANES:])
        return jnp.concatenate([moved[:, :ny - LANES], tail], axis=1)

    def edge_of(halo, l, r):
        return halo[l * nx + r:l * nx + r + ROWS]

    sheets = [sheet_ref[here["gz"] * lay + l] for l in range(lay)]
    classes = table_ref.shape[0]

    def look_up(label, l):
        value = jnp.full(label.shape, sheets[l] * table_ref[classes - 1], F32)
        for c in range(classes - 1):
            value = jnp.where(label == c, sheets[l] * table_ref[c], value)
        return value

    loads[0].wait()
    for l, r in chunks:
        cond_x[l, PAD + r:PAD + r + ROWS, :] = look_up(class_x[l, r:r + ROWS, :], l)

    @pl.when(at_end("gx", 1))
    def _():
        cond_x[:, last, :] = jnp.zeros((lay, ny), F32)

    loads[1].wait()
    for l, r in chunks:
        cond_y[l, r:r + ROWS, :] = look_up(class_y[l, r:r + ROWS, :], l)

    @pl.when(at_end("gy", 1))
    def _():
        for l in range(lay):
            tile = cond_y[l, :, ny - LANES:]
            spot = lax.broadcasted_iota(jnp.int32, tile.shape, 1)
            cond_y[l, :, ny - LANES:] = jnp.where(spot == LANES - 1, 0.0, tile)

    row_send[ROW["cx"]] = cond_x[:, last, :]
    put_col("cy", cond_y[:, :, ny - LANES:], LANES - 1)
    loads[2].wait()
    loads[3].wait()
    loads[4].wait()
    row_send[ROW["vx"]] = volt[:, first, :]
    put_col("vy", volt[:, inner, :LANES], 0)
    pl.semaphore_wait(barrier, group - 1)
    send("cv", "cx", "cy", "vx", "vy", "vl")
    receive("cx", "cy", "cv")

    cond_x[:, PAD - 1, :] = row_recv[ROW["cx"]]
    halo = col_halo("cy")
    moment0 = jnp.zeros((ROWS, ny), F32)
    for l, r in chunks:
        rows = slice(r, r + ROWS)
        cy = cond_y[l, rows, :]
        ly = from_left(cy, edge_of(halo, l, r))
        low_y[l, rows, :] = ly
        below = via[l - 1, rows, :] if l > 0 else lay_recv[LAY["cv"], rows, :]
        total = (cond_x[l, PAD + r:PAD + r + ROWS, :] + cond_x[l, PAD - 1 + r:PAD - 1 + r + ROWS, :]
                 + cy + ly + via[l, rows, :] + below)
        inv = 1.0 / total
        inverse[l, rows, :] = inv
        value = source[l, rows, :] * inv
        z[l, PAD + r:PAD + r + ROWS, :] = value
        moment0 = moment0 + source[l, rows, :] * value
    row_send[ROW["zx_up"]] = z[:, last, :]
    put_col("zy_up", z[:, inner, ny - LANES:], LANES - 1)
    send("zl_up", "zl_dn", "zx_up", "zy_up")

    one = lane[0:1]

    def from_left_row(value):
        moved = pltpu.roll(value, 1, 1)
        return jnp.concatenate([jnp.where(one == 0, 0.0, moved[:, :LANES]), moved[:, LANES:]], axis=1)

    def from_right_row(value):
        moved = pltpu.roll(value, ny - 1, 1)
        tail = jnp.where(one == LANES - 1, 0.0, moved[:, ny - LANES:])
        return jnp.concatenate([moved[:, :ny - LANES], tail], axis=1)

    col_parts = []
    for l in range(lay):
        row = z[l, first:first + 1, :]
        s = cond_x[l, first:first + 1, :] * z[l, first + 1:first + 2, :]
        s = s + cond_y[l, 0:1, :] * from_right_row(row) + low_y[l, 0:1, :] * from_left_row(row)
        tile = z[l, inner, :LANES]
        c = cond_x[l, inner, :LANES] * z[l, PAD + 1:PAD + 1 + nx, :LANES]
        c = c + cond_x[l, PAD - 1:PAD - 1 + nx, :LANES] * z[l, PAD - 1:PAD - 1 + nx, :LANES]
        c = c + cond_y[l, :, :LANES] * pltpu.roll(tile, LANES - 1, 1)
        if l + 1 < lay:
            s = s + via[l, 0:1, :] * z[l + 1, first:first + 1, :]
            c = c + via[l, :, :LANES] * z[l + 1, inner, :LANES]
        if l > 0:
            s = s + via[l - 1, 0:1, :] * z[l - 1, first:first + 1, :]
            c = c + via[l - 1, :, :LANES] * z[l - 1, inner, :LANES]
        xd_send[l:l + 1, :] = row
        xd_send[lay + l:lay + l + 1, :] = s
        xd_send[2 * lay + l:2 * lay + l + 1, :] = inverse[l, 0:1, :]
        col_parts.append(c)
    yd_send[0:1, :] = as_row(z[:, inner, :LANES], 0)
    yd_send[1:2, :] = as_row(jnp.stack(col_parts), 0)
    yd_send[2:3, :] = as_row(inverse[:, :, :LANES], 0)
    top = lay - 1
    over_send[0] = via[top, 0:1, :] * z[top, first:first + 1, :]
    over_send[1] = lay_recv[LAY["cv"], 0:1, :] * z[0, first:first + 1, :]
    blank = [jnp.zeros((nx, LANES), F32)] * (lay - 1)
    put_col("ly_up", jnp.stack([via[top, :, :LANES] * z[top, inner, :LANES]] + blank), 0)
    put_col("ly_dn", jnp.stack(blank + [lay_recv[LAY["cv"], :, :LANES] * z[0, inner, :LANES]]), 0)
    for l in range(lay):
        row = z[l, first:first + 1, :]
        tail = cond_y[l, 0:1, ny - LANES:] * row[:, ny - LANES:]
        row_end_send[0, l:l + 1, :] = jnp.where(one == 0, pltpu.roll(tail, 1, 1), 0.0)
        head = low_y[l, 0:1, :LANES] * row[:, :LANES]
        row_end_send[1, l:l + 1, :] = jnp.where(one == LANES - 1, pltpu.roll(head, LANES - 1, 1), 0.0)
        head = cond_x[l, PAD - 1:PAD, :LANES] * row[:, :LANES]
        col_end_send[0, l:l + 1, :] = jnp.broadcast_to(head[:, :1], (1, lay * nx))
        head = cond_x[l, last:last + 1, :LANES] * z[l, last:last + 1, :LANES]
        col_end_send[1, l:l + 1, :] = jnp.broadcast_to(head[:, :1], (1, lay * nx))
    send("xd", "yd", "lx_up", "lx_dn", "ly_up", "ly_dn", "ca", "cb", "cc", "cd")

    receive("vx", "vy", "vl")
    volt[:, last + 1, :] = row_recv[ROW["vx"]]
    halo = col_halo("vy")
    for l, r in chunks:
        rows = slice(r, r + ROWS)
        v = volt[l, PAD + r:PAD + r + ROWS, :]
        above = volt[l + 1, PAD + r:PAD + r + ROWS, :] if l + 1 < lay else lay_recv[LAY["vl"], rows, :]
        grad_x_ref[l, rows, :] = -sheets[l] * (v - volt[l, PAD + 1 + r:PAD + 1 + r + ROWS, :])
        grad_y_ref[l, rows, :] = -sheets[l] * (v - from_right(v, edge_of(halo, l, r)))
        grad_v_ref[l, rows, :] = above - v

    @pl.when(at_end("gx", 1))
    def _():
        grad_x_ref[:, nx - 1, :] = jnp.zeros((lay, ny), F32)

    @pl.when(at_end("gy", 1))
    def _():
        for l in range(lay):
            tile = grad_y_ref[l, :, ny - LANES:]
            spot = lax.broadcasted_iota(jnp.int32, tile.shape, 1)
            grad_y_ref[l, :, ny - LANES:] = jnp.where(spot == LANES - 1, 0.0, tile)

    receive("zx_up", "zy_up", "zl_up", "zl_dn", "xd", "yd")
    z[:, PAD - 1, :] = row_recv[ROW["zx_up"]]
    z[:, last + 1, :] = xd_recv[:lay, :]
    halo_lo = col_halo("zy_up")
    halo_hi = as_col(yd_recv[0:1, :])
    moment1 = jnp.zeros((ROWS, ny), F32)
    moment2 = jnp.zeros((ROWS, ny), F32)
    for l, r in chunks:
        rows = slice(r, r + ROWS)
        mid = slice(PAD + r, PAD + r + ROWS)
        lower = slice(PAD - 1 + r, PAD - 1 + r + ROWS)
        upper = slice(PAD + 1 + r, PAD + 1 + r + ROWS)
        here_z = z[l, mid, :]
        z_above = z[l + 1, mid, :] if l + 1 < lay else lay_recv[LAY["zl_dn"], rows, :]
        z_below = z[l - 1, mid, :] if l > 0 else lay_recv[LAY["zl_up"], rows, :]
        below = via[l - 1, rows, :] if l > 0 else lay_recv[LAY["cv"], rows, :]
        s = cond_x[l, mid, :] * z[l, upper, :] + cond_x[l, lower, :] * z[l, lower, :]
        s = s + cond_y[l, rows, :] * from_right(here_z, edge_of(halo_hi, l, r))
        s = s + low_y[l, rows, :] * from_left(here_z, edge_of(halo_lo, l, r))
        s = s + via[l, rows, :] * z_above + below * z_below
        value = s * inverse[l, rows, :]
        t[l, mid, :] = value
        moment1 = moment1 + here_z * s
        moment2 = moment2 + value * s
    send("tl")

    receive("lx_up", "lx_dn", "ly_up", "ly_dn", "ca", "cb", "cc", "cd")
    for l in range(lay):
        s = xd_recv[lay + l:lay + l + 1, :] + cond_x[l, last:last + 1, :] * z[l, last:last + 1, :]
        if l == 0:
            s = s + over_recv[0]
        if l == lay - 1:
            s = s + over_recv[1]
        s = jnp.concatenate(
            [s[:, :LANES] + row_end_recv[0, l:l + 1, :], s[:, LANES:ny - LANES],
             s[:, ny - LANES:] + row_end_recv[1, l:l + 1, :]], axis=1)
        t[l, last + 1:last + 2, :] = s * xd_recv[2 * lay + l:2 * lay + l + 1, :]
    s = yd_recv[1:2, :] + col_send[COL["cy"]] * col_send[COL["zy_up"]]
    s = s + col_recv[COL["ly_up"]] + col_recv[COL["ly_dn"]]
    spot = lax.broadcasted_iota(jnp.int32, (1, lay * nx), 1)
    for l in range(lay):
        s = s + jnp.where(spot == l * nx + nx - 1, col_end_recv[0, l:l + 1, :], 0.0)
        s = s + jnp.where(spot == l * nx, col_end_recv[1, l:l + 1, :], 0.0)
    halo_t = as_col(s * yd_recv[2:3, :])
    receive("tl")
    moment3 = jnp.zeros((ROWS, ny), F32)
    for l, r in chunks:
        rows = slice(r, r + ROWS)
        mid = slice(PAD + r, PAD + r + ROWS)
        upper = slice(PAD + 1 + r, PAD + 1 + r + ROWS)
        here_t = t[l, mid, :]
        t_above = t[l + 1, mid, :] if l + 1 < lay else lay_recv[LAY["tl"], rows, :]
        s = cond_x[l, mid, :] * t[l, upper, :]
        s = s + cond_y[l, rows, :] * from_right(here_t, edge_of(halo_t, l, r))
        s = s + via[l, rows, :] * t_above
        moment3 = moment3 + here_t * s

    def fold(value):
        wide = sum(value[:, k:k + LANES] for k in range(0, ny, LANES))
        return jnp.sum(wide, axis=0, keepdims=True)

    part[0:1, :] = fold(moment0)
    part[1:2, :] = fold(moment1)
    part[2:3, :] = fold(moment2)
    part[3:4, :] = 2.0 * fold(moment3)
    part[4:8, :] = jnp.zeros((4, LANES), F32)

    def share(peer, slot):
        return pltpu.make_async_remote_copy(
            src_ref=part, dst_ref=parts.at[slot], send_sem=part_send.at[peer], recv_sem=part_recv.at[slot],
            device_id=place(peer), device_id_type=pl.DeviceIdType.MESH)

    each_peer(lambda peer: share(peer, me).start())
    parts[me] = part[...]
    each_peer(lambda peer: share(peer, peer).wait_recv())
    totals = jnp.sum(jnp.sum(parts[...], axis=0), axis=1, keepdims=True)
    c0, c1, c2, c3 = (totals[k:k + 1, :] for k in range(4))
    curve = c0 - c1
    alpha = c0 / curve
    rest = -c1 / curve
    rho = rest * rest * c0 + 2.0 * rest * alpha * c1 + alpha * alpha * c2
    beta = rho / c0
    cross = rest * curve + alpha * (c1 - c2)
    own = rest * rest * curve + 2.0 * rest * alpha * (c1 - c2) + alpha * alpha * (c2 - c3)
    alpha_next = rho / (own + 2.0 * beta * cross + beta * beta * curve)
    factor_z = jnp.broadcast_to(alpha + alpha_next * (rest + beta), (1, ny))
    factor_t = jnp.broadcast_to(alpha_next * alpha, (1, ny))

    adj[:, last + 1, :] = factor_z * z[:, last + 1, :] + factor_t * t[:, last + 1, :]
    for l, r in chunks:
        mid = slice(PAD + r, PAD + r + ROWS)
        value = factor_z * z[l, mid, :] + factor_t * t[l, mid, :]
        adj[l, mid, :] = value
        adj_ref[l, r:r + ROWS, :] = value
    halo = factor_z[:, :LANES] * halo_hi + factor_t[:, :LANES] * halo_t
    for l, r in chunks:
        rows = slice(r, r + ROWS)
        mid = slice(PAD + r, PAD + r + ROWS)
        upper = slice(PAD + 1 + r, PAD + 1 + r + ROWS)
        value = adj[l, mid, :]
        if l + 1 < lay:
            above = adj[l + 1, mid, :]
        else:
            above = factor_z * lay_recv[LAY["zl_dn"], rows, :] + factor_t * lay_recv[LAY["tl"], rows, :]
        grad_x_ref[l, rows, :] = grad_x_ref[l, rows, :] * (value - adj[l, upper, :])
        grad_y_ref[l, rows, :] = grad_y_ref[l, rows, :] * (value - from_right(value, edge_of(halo, l, r)))
        grad_v_ref[l, rows, :] = grad_v_ref[l, rows, :] * (value - above)

    sent(*NAMES)
    each_peer(lambda peer: share(peer, me).wait_send())


def write_out(*refs):
    sem = refs[-1]
    copies = [pltpu.make_async_copy(refs[i], refs[4 + i], sem.at[i]) for i in range(4)]
    for copy in copies:
        copy.start()
    for copy in copies:
        copy.wait()


def body(sizes, *args):
    lay, nx, ny = args[0].shape
    group = sizes["gx"] * sizes["gy"] * sizes["gz"]
    block = jax.ShapeDtypeStruct((lay, nx, ny), F32)
    whole = pl.BlockSpec(memory_space=pltpu.HBM)
    scalars = pl.BlockSpec(memory_space=pltpu.SMEM)
    vmem = pl.BlockSpec(memory_space=pltpu.VMEM)
    flat = lambda dtype=F32: pltpu.VMEM((lay, nx, ny), dtype)
    tall = pltpu.VMEM((lay, nx + 2 * PAD, ny), F32)
    args = [pltpu.with_memory_space_constraint(a, pltpu.HBM) for a in args]
    results = pl.pallas_call(
        functools.partial(kernel, sizes, (lay, nx, ny)),
        out_shape=(block,) * 4,
        in_specs=[whole] * 5 + [scalars] * 2,
        out_specs=(vmem,) * 4,
        scratch_shapes=[
            flat(), tall, flat(jnp.int32), flat(jnp.int32), flat(),
            tall, flat(), flat(), flat(), tall, tall, tall,
            pltpu.VMEM((3, lay, ny), F32), pltpu.VMEM((3, lay, ny), F32),
            pltpu.VMEM((5, 1, lay * nx), F32), pltpu.VMEM((5, 1, lay * nx), F32),
            pltpu.VMEM((5, nx, ny), F32),
            pltpu.VMEM((3 * lay, ny), F32), pltpu.VMEM((3 * lay, ny), F32),
            pltpu.VMEM((3, lay * nx), F32), pltpu.VMEM((3, lay * nx), F32),
            pltpu.VMEM((2, 1, ny), F32), pltpu.VMEM((2, 1, ny), F32),
            pltpu.VMEM((2, lay, LANES), F32), pltpu.VMEM((2, lay, LANES), F32),
            pltpu.VMEM((2, lay, lay * nx), F32), pltpu.VMEM((2, lay, lay * nx), F32),
            pltpu.VMEM((8, LANES), F32), pltpu.VMEM((group, 8, LANES), F32),
            pltpu.SemaphoreType.DMA((5,)),
            pltpu.SemaphoreType.DMA((len(NAMES),)), pltpu.SemaphoreType.DMA((len(NAMES),)),
            pltpu.SemaphoreType.DMA((group,)), pltpu.SemaphoreType.DMA((group,)),
        ],
        compiler_params=pltpu.CompilerParams(
            collective_id=0, has_side_effects=True, vmem_limit_bytes=32 * 1024 * 1024),
    )(*args)
    return pl.pallas_call(
        write_out,
        out_shape=(block,) * 4,
        in_specs=[pl.BlockSpec(memory_space=pl.ANY)] * 4, compiler_params=pltpu.CompilerParams(vmem_limit_bytes=1024*1024),
        out_specs=(whole,) * 4,
        scratch_shapes=[pltpu.SemaphoreType.DMA((4,))],
    )(*results)


def solution(mesh):
    placed = P(("parts", "gz"), "gx", "gy")
    sizes = {axis: mesh.shape[axis] for axis in ("gx", "gy", "gz")}
    return jax.shard_map(
        functools.partial(body, sizes),
        mesh=mesh,
        in_specs=(placed,) * 5 + (P(), P()),
        out_specs=(placed,) * 4,
        check_vma=False,
    )
```

```python
import functools

import jax
import jax.numpy as jnp
from jax import lax
from jax.experimental import pallas as pl
from jax.experimental.pallas import tpu as pltpu
from jax.sharding import PartitionSpec as P

F32 = jnp.float32
PAD = 8
ROWS = 16
LANES = 128
MESSAGES = {
    "cx": {"gx": 1}, "cy": {"gy": 1}, "cv": {"gz": 1},
    "vx": {"gx": -1}, "vy": {"gy": -1}, "vl": {"gz": -1},
    "zx_up": {"gx": 1}, "zy_up": {"gy": 1}, "zl_up": {"gz": 1}, "zl_dn": {"gz": -1},
    "xd": {"gx": -1}, "yd": {"gy": -1}, "tl": {"gz": -1},
    "lx_up": {"gx": -1, "gz": 1}, "lx_dn": {"gx": -1, "gz": -1},
    "ly_up": {"gy": -1, "gz": 1}, "ly_dn": {"gy": -1, "gz": -1},
    "ca": {"gx": -1, "gy": 1}, "cb": {"gx": -1, "gy": -1}, "cc": {"gx": -1, "gy": -1},
    "cd": {"gx": 1, "gy": -1},
}
NAMES = list(MESSAGES)


def kernel(
    sizes, dims,
    source_hbm, volt_hbm, class_x_hbm, class_y_hbm, via_hbm, sheet_ref, table_ref,
    adj_ref, grad_x_ref, grad_y_ref, grad_v_ref,
    source, volt, class_x, class_y, via, cond_x, cond_y, low_y, inverse, z, t, of_t,
    row_send, row_recv, col_send, col_recv, lay_recv,
    xd_send, xd_recv, yd_send, yd_recv, over_send, over_recv, row_end_send, row_end_recv,
    col_end_send, col_end_recv, part, parts,
    load_sem, send_sem, recv_sem, part_send, part_recv,
):
    lay, nx, ny = dims
    group = sizes["gx"] * sizes["gy"] * sizes["gz"]
    here = {axis: lax.axis_index(axis) for axis in ("gx", "gy", "gz")}
    me = (here["gx"] * sizes["gy"] + here["gy"]) * sizes["gz"] + here["gz"]
    inner = pl.ds(PAD, nx)
    first, last = PAD, PAD + nx - 1

    loads = []
    for i, (src, dst) in enumerate((
        (class_x_hbm, class_x), (class_y_hbm, class_y), (via_hbm, via),
        (source_hbm, source), (volt_hbm, volt.at[:, inner, :]),
    )):
        copy = pltpu.make_async_copy(src, dst, load_sem.at[i])
        copy.start()
        loads.append(copy)

    row_recv[...] = jnp.zeros_like(row_recv)
    col_recv[...] = jnp.zeros_like(col_recv)
    for ref in (xd_recv, yd_recv, over_recv, row_end_recv, col_end_recv):
        ref[...] = jnp.zeros_like(ref)
    z[:, PAD - 1, :] = jnp.zeros((lay, ny), F32)
    z[:, last + 1, :] = jnp.zeros((lay, ny), F32)

    empty = jnp.zeros((nx, ny), F32)

    @pl.when(here["gz"] == sizes["gz"] - 1)
    def _():
        for slot in (1, 3, 4):
            lay_recv[slot] = empty

    @pl.when(here["gz"] == 0)
    def _():
        for slot in (0, 2):
            lay_recv[slot] = empty

    def place(rank):
        gz = lax.rem(rank, sizes["gz"])
        rest = lax.div(rank, sizes["gz"])
        return {"gx": lax.div(rest, sizes["gy"]), "gy": lax.rem(rest, sizes["gy"]), "gz": gz}

    barrier = pltpu.get_barrier_semaphore()

    def each_peer(body):
        if group <= 32:
            for k in range(1, group):
                body(lax.rem(me + k, group))
        else:
            lax.fori_loop(1, group, lambda k, c: (body(lax.rem(me + k, group)), c)[1], 0)

    each_peer(lambda peer: pl.semaphore_signal(
        barrier, inc=1, device_id=place(peer), device_id_type=pl.DeviceIdType.MESH))

    ROW = {"cx": 0, "vx": 1, "zx_up": 2}
    COL = {"cy": 0, "vy": 1, "zy_up": 2, "ly_up": 3, "ly_dn": 4}
    LAY = {"cv": 0, "vl": 1, "zl_up": 2, "zl_dn": 3, "tl": 4}
    LAY_SRC = {
        "cv": via.at[lay - 1], "vl": volt.at[0, inner, :], "zl_up": z.at[lay - 1, inner, :],
        "zl_dn": z.at[0, inner, :], "tl": t.at[0, inner, :],
    }

    OTHER = {
        "xd": (xd_send, xd_recv), "yd": (yd_send, yd_recv),
        "lx_up": (over_send.at[0], over_recv.at[0]), "lx_dn": (over_send.at[1], over_recv.at[1]),
        "ca": (row_end_send.at[0], row_end_recv.at[0]), "cb": (row_end_send.at[1], row_end_recv.at[1]),
        "cc": (col_end_send.at[0], col_end_recv.at[0]), "cd": (col_end_send.at[1], col_end_recv.at[1]),
    }

    def message(name):
        i = NAMES.index(name)
        if name in ROW:
            src, dst = row_send.at[ROW[name]], row_recv.at[ROW[name]]
        elif name in COL:
            src, dst = col_send.at[COL[name]], col_recv.at[COL[name]]
        elif name in OTHER:
            src, dst = OTHER[name]
        else:
            src, dst = LAY_SRC[name], lay_recv.at[LAY[name]]
        to = {axis: lax.rem(here[axis] + (way + sizes[axis]), sizes[axis])
              for axis, way in MESSAGES[name].items()}
        return pltpu.make_async_remote_copy(
            src_ref=src, dst_ref=dst, send_sem=send_sem.at[i], recv_sem=recv_sem.at[i],
            device_id=to, device_id_type=pl.DeviceIdType.MESH)

    def at_end(axis, way):
        return here[axis] == (sizes[axis] - 1 if way > 0 else 0)

    def guarded(name, sign, action):
        ways = MESSAGES[name]
        if any(sizes[axis] == 1 for axis in ways):
            return
        inside = [jnp.logical_not(at_end(axis, sign * way)) for axis, way in ways.items()]
        pl.when(functools.reduce(jnp.logical_and, inside))(action)

    def send(*names):
        for name in names:
            guarded(name, 1, message(name).start)

    def receive(*names):
        for name in names:
            guarded(name, -1, message(name).wait_recv)

    def sent(*names):
        for name in names:
            guarded(name, 1, message(name).wait_send)

    chunks = [(l, r) for l in range(lay) for r in range(0, nx, ROWS)]
    lane = lax.broadcasted_iota(jnp.int32, (ROWS, LANES), 1)

    def as_row(tile, at):
        return tile.reshape(lay * nx, LANES).T[at:at + 1, :]

    def put_col(name, tile, at):
        col_send[COL[name]] = as_row(tile, at)

    def as_col(row):
        return jnp.broadcast_to(row, (LANES, lay * nx)).T

    def col_halo(name):
        return as_col(col_recv[COL[name]])

    def from_left(value, edge):
        moved = pltpu.roll(value, 1, 1)
        head = jnp.where(lane == 0, edge, moved[:, :LANES])
        return jnp.concatenate([head, moved[:, LANES:]], axis=1)

    def from_right(value, edge):
        moved = pltpu.roll(value, ny - 1, 1)
        tail = jnp.where(lane == LANES - 1, edge, moved[:, ny - LANES:])
        return jnp.concatenate([moved[:, :ny - LANES], tail], axis=1)

    def edge_of(halo, l, r):
        return halo[l * nx + r:l * nx + r + ROWS]

    sheets = [sheet_ref[here["gz"] * lay + l] for l in range(lay)]
    classes = table_ref.shape[0]

    def look_up(label, l):
        value = jnp.full(label.shape, sheets[l] * table_ref[classes - 1], F32)
        for c in range(classes - 1):
            value = jnp.where(label == c, sheets[l] * table_ref[c], value)
        return value

    loads[0].wait()
    for l, r in chunks:
        cond_x[l, PAD + r:PAD + r + ROWS, :] = look_up(class_x[l, r:r + ROWS, :], l)

    @pl.when(at_end("gx", 1))
    def _():
        cond_x[:, last, :] = jnp.zeros((lay, ny), F32)

    loads[1].wait()
    for l, r in chunks:
        cond_y[l, r:r + ROWS, :] = look_up(class_y[l, r:r + ROWS, :], l)

    @pl.when(at_end("gy", 1))
    def _():
        for l in range(lay):
            tile = cond_y[l, :, ny - LANES:]
            spot = lax.broadcasted_iota(jnp.int32, tile.shape, 1)
            cond_y[l, :, ny - LANES:] = jnp.where(spot == LANES - 1, 0.0, tile)

    row_send[ROW["cx"]] = cond_x[:, last, :]
    put_col("cy", cond_y[:, :, ny - LANES:], LANES - 1)
    loads[2].wait()
    loads[3].wait()
    loads[4].wait()
    row_send[ROW["vx"]] = volt[:, first, :]
    put_col("vy", volt[:, inner, :LANES], 0)
    pl.semaphore_wait(barrier, group - 1)
    send("cv", "cx", "cy", "vx", "vy", "vl")
    receive("cx", "cy", "cv")

    cond_x[:, PAD - 1, :] = row_recv[ROW["cx"]]
    halo = col_halo("cy")
    moment0 = jnp.zeros((ROWS, ny), F32)
    for l, r in chunks:
        rows = slice(r, r + ROWS)
        cy = cond_y[l, rows, :]
        ly = from_left(cy, edge_of(halo, l, r))
        low_y[l, rows, :] = ly
        below = via[l - 1, rows, :] if l > 0 else lay_recv[LAY["cv"], rows, :]
        total = (cond_x[l, PAD + r:PAD + r + ROWS, :] + cond_x[l, PAD - 1 + r:PAD - 1 + r + ROWS, :]
                 + cy + ly + via[l, rows, :] + below)
        inv = 1.0 / total
        inverse[l, rows, :] = inv
        value = source[l, rows, :] * inv
        z[l, PAD + r:PAD + r + ROWS, :] = value
        moment0 = moment0 + source[l, rows, :] * value
    row_send[ROW["zx_up"]] = z[:, last, :]
    put_col("zy_up", z[:, inner, ny - LANES:], LANES - 1)
    send("zl_up", "zl_dn", "zx_up", "zy_up")

    one = lane[0:1]

    def from_left_row(value):
        moved = pltpu.roll(value, 1, 1)
        return jnp.concatenate([jnp.where(one == 0, 0.0, moved[:, :LANES]), moved[:, LANES:]], axis=1)

    def from_right_row(value):
        moved = pltpu.roll(value, ny - 1, 1)
        tail = jnp.where(one == LANES - 1, 0.0, moved[:, ny - LANES:])
        return jnp.concatenate([moved[:, :ny - LANES], tail], axis=1)

    col_parts = []
    for l in range(lay):
        row = z[l, first:first + 1, :]
        s = cond_x[l, first:first + 1, :] * z[l, first + 1:first + 2, :]
        s = s + cond_y[l, 0:1, :] * from_right_row(row) + low_y[l, 0:1, :] * from_left_row(row)
        tile = z[l, inner, :LANES]
        c = cond_x[l, inner, :LANES] * z[l, PAD + 1:PAD + 1 + nx, :LANES]
        c = c + cond_x[l, PAD - 1:PAD - 1 + nx, :LANES] * z[l, PAD - 1:PAD - 1 + nx, :LANES]
        c = c + cond_y[l, :, :LANES] * pltpu.roll(tile, LANES - 1, 1)
        if l + 1 < lay:
            s = s + via[l, 0:1, :] * z[l + 1, first:first + 1, :]
            c = c + via[l, :, :LANES] * z[l + 1, inner, :LANES]
        if l > 0:
            s = s + via[l - 1, 0:1, :] * z[l - 1, first:first + 1, :]
            c = c + via[l - 1, :, :LANES] * z[l - 1, inner, :LANES]
        xd_send[l:l + 1, :] = row
        xd_send[lay + l:lay + l + 1, :] = s
        xd_send[2 * lay + l:2 * lay + l + 1, :] = inverse[l, 0:1, :]
        col_parts.append(c)
    yd_send[0:1, :] = as_row(z[:, inner, :LANES], 0)
    yd_send[1:2, :] = as_row(jnp.stack(col_parts), 0)
    yd_send[2:3, :] = as_row(inverse[:, :, :LANES], 0)
    top = lay - 1
    over_send[0] = via[top, 0:1, :] * z[top, first:first + 1, :]
    over_send[1] = lay_recv[LAY["cv"], 0:1, :] * z[0, first:first + 1, :]
    blank = [jnp.zeros((nx, LANES), F32)] * (lay - 1)
    put_col("ly_up", jnp.stack([via[top, :, :LANES] * z[top, inner, :LANES]] + blank), 0)
    put_col("ly_dn", jnp.stack(blank + [lay_recv[LAY["cv"], :, :LANES] * z[0, inner, :LANES]]), 0)
    for l in range(lay):
        row = z[l, first:first + 1, :]
        tail = cond_y[l, 0:1, ny - LANES:] * row[:, ny - LANES:]
        row_end_send[0, l:l + 1, :] = jnp.where(one == 0, pltpu.roll(tail, 1, 1), 0.0)
        head = low_y[l, 0:1, :LANES] * row[:, :LANES]
        row_end_send[1, l:l + 1, :] = jnp.where(one == LANES - 1, pltpu.roll(head, LANES - 1, 1), 0.0)
        head = cond_x[l, PAD - 1:PAD, :LANES] * row[:, :LANES]
        col_end_send[0, l:l + 1, :] = jnp.broadcast_to(head[:, :1], (1, lay * nx))
        head = cond_x[l, last:last + 1, :LANES] * z[l, last:last + 1, :LANES]
        col_end_send[1, l:l + 1, :] = jnp.broadcast_to(head[:, :1], (1, lay * nx))
    send("xd", "yd", "lx_up", "lx_dn", "ly_up", "ly_dn", "ca", "cb", "cc", "cd")

    receive("vx", "vy", "vl")
    volt[:, last + 1, :] = row_recv[ROW["vx"]]
    halo = col_halo("vy")
    for l, r in chunks:
        rows = slice(r, r + ROWS)
        v = volt[l, PAD + r:PAD + r + ROWS, :]
        above = volt[l + 1, PAD + r:PAD + r + ROWS, :] if l + 1 < lay else lay_recv[LAY["vl"], rows, :]
        grad_x_ref[l, rows, :] = -sheets[l] * (v - volt[l, PAD + 1 + r:PAD + 1 + r + ROWS, :])
        grad_y_ref[l, rows, :] = -sheets[l] * (v - from_right(v, edge_of(halo, l, r)))
        grad_v_ref[l, rows, :] = above - v

    @pl.when(at_end("gx", 1))
    def _():
        grad_x_ref[:, nx - 1, :] = jnp.zeros((lay, ny), F32)

    @pl.when(at_end("gy", 1))
    def _():
        for l in range(lay):
            tile = grad_y_ref[l, :, ny - LANES:]
            spot = lax.broadcasted_iota(jnp.int32, tile.shape, 1)
            grad_y_ref[l, :, ny - LANES:] = jnp.where(spot == LANES - 1, 0.0, tile)

    receive("zx_up", "zy_up", "zl_up", "zl_dn", "xd", "yd")
    z[:, PAD - 1, :] = row_recv[ROW["zx_up"]]
    z[:, last + 1, :] = xd_recv[:lay, :]
    halo_lo = col_halo("zy_up")
    halo_hi = as_col(yd_recv[0:1, :])
    moment1 = jnp.zeros((ROWS, ny), F32)
    moment2 = jnp.zeros((ROWS, ny), F32)
    for l, r in chunks:
        rows = slice(r, r + ROWS)
        mid = slice(PAD + r, PAD + r + ROWS)
        lower = slice(PAD - 1 + r, PAD - 1 + r + ROWS)
        upper = slice(PAD + 1 + r, PAD + 1 + r + ROWS)
        here_z = z[l, mid, :]
        z_above = z[l + 1, mid, :] if l + 1 < lay else lay_recv[LAY["zl_dn"], rows, :]
        z_below = z[l - 1, mid, :] if l > 0 else lay_recv[LAY["zl_up"], rows, :]
        below = via[l - 1, rows, :] if l > 0 else lay_recv[LAY["cv"], rows, :]
        s = cond_x[l, mid, :] * z[l, upper, :] + cond_x[l, lower, :] * z[l, lower, :]
        s = s + cond_y[l, rows, :] * from_right(here_z, edge_of(halo_hi, l, r))
        s = s + low_y[l, rows, :] * from_left(here_z, edge_of(halo_lo, l, r))
        s = s + via[l, rows, :] * z_above + below * z_below
        value = s * inverse[l, rows, :]
        t[l, mid, :] = value
        moment1 = moment1 + here_z * s
        moment2 = moment2 + value * s
        if l == 0 and r + ROWS == nx:
            send("tl")

    receive("lx_up", "lx_dn", "ly_up", "ly_dn", "ca", "cb", "cc", "cd")
    for l in range(lay):
        s = xd_recv[lay + l:lay + l + 1, :] + cond_x[l, last:last + 1, :] * z[l, last:last + 1, :]
        if l == 0:
            s = s + over_recv[0]
        if l == lay - 1:
            s = s + over_recv[1]
        s = jnp.concatenate(
            [s[:, :LANES] + row_end_recv[0, l:l + 1, :], s[:, LANES:ny - LANES],
             s[:, ny - LANES:] + row_end_recv[1, l:l + 1, :]], axis=1)
        t[l, last + 1:last + 2, :] = s * xd_recv[2 * lay + l:2 * lay + l + 1, :]
    s = yd_recv[1:2, :] + col_send[COL["cy"]] * col_send[COL["zy_up"]]
    s = s + col_recv[COL["ly_up"]] + col_recv[COL["ly_dn"]]
    spot = lax.broadcasted_iota(jnp.int32, (1, lay * nx), 1)
    for l in range(lay):
        s = s + jnp.where(spot == l * nx + nx - 1, col_end_recv[0, l:l + 1, :], 0.0)
        s = s + jnp.where(spot == l * nx, col_end_recv[1, l:l + 1, :], 0.0)
    halo_t = as_col(s * yd_recv[2:3, :])
    moment3 = jnp.zeros((ROWS, ny), F32)
    for l, r in chunks:
        rows = slice(r, r + ROWS)
        mid = slice(PAD + r, PAD + r + ROWS)
        upper = slice(PAD + 1 + r, PAD + 1 + r + ROWS)
        here_t = t[l, mid, :]
        s = cond_x[l, mid, :] * t[l, upper, :]
        s = s + cond_y[l, rows, :] * from_right(here_t, edge_of(halo_t, l, r))
        if l + 1 < lay:
            s = s + via[l, rows, :] * t[l + 1, mid, :]
        moment3 = moment3 + here_t * s
    receive("tl")
    for r in range(0, nx, ROWS):
        rows = slice(r, r + ROWS)
        s = via[lay - 1, rows, :] * lay_recv[LAY["tl"], rows, :]
        moment3 = moment3 + t[lay - 1, PAD + r:PAD + r + ROWS, :] * s

    def fold(value):
        wide = sum(value[:, k:k + LANES] for k in range(0, ny, LANES))
        return jnp.sum(wide, axis=0, keepdims=True)

    part[0:1, :] = fold(moment0)
    part[1:2, :] = fold(moment1)
    part[2:3, :] = fold(moment2)
    part[3:4, :] = 2.0 * fold(moment3)
    part[4:8, :] = jnp.zeros((4, LANES), F32)

    def share(peer, slot):
        return pltpu.make_async_remote_copy(
            src_ref=part, dst_ref=parts.at[slot], send_sem=part_send.at[peer], recv_sem=part_recv.at[slot],
            device_id=place(peer), device_id_type=pl.DeviceIdType.MESH)

    each_peer(lambda peer: share(peer, me).start())
    parts[me] = part[...]

    for l, r in chunks:
        rows = slice(r, r + ROWS)
        mid = slice(PAD + r, PAD + r + ROWS)
        upper = slice(PAD + 1 + r, PAD + 1 + r + ROWS)
        here_z, here_t = z[l, mid, :], t[l, mid, :]
        if l + 1 < lay:
            z_above, t_above = z[l + 1, mid, :], t[l + 1, mid, :]
        else:
            z_above, t_above = lay_recv[LAY["zl_dn"], rows, :], lay_recv[LAY["tl"], rows, :]
        volts = grad_x_ref[l, rows, :]
        grad_x_ref[l, rows, :] = volts * (here_z - z[l, upper, :])
        of_t[0, l, rows, :] = volts * (here_t - t[l, upper, :])
        volts = grad_y_ref[l, rows, :]
        grad_y_ref[l, rows, :] = volts * (here_z - from_right(here_z, edge_of(halo_hi, l, r)))
        of_t[1, l, rows, :] = volts * (here_t - from_right(here_t, edge_of(halo_t, l, r)))
        volts = grad_v_ref[l, rows, :]
        grad_v_ref[l, rows, :] = volts * (here_z - z_above)
        of_t[2, l, rows, :] = volts * (here_t - t_above)

    each_peer(lambda peer: share(peer, peer).wait_recv())
    totals = jnp.sum(jnp.sum(parts[...], axis=0), axis=1, keepdims=True)
    c0, c1, c2, c3 = (totals[k:k + 1, :] for k in range(4))
    curve = c0 - c1
    alpha = c0 / curve
    rest = -c1 / curve
    rho = rest * rest * c0 + 2.0 * rest * alpha * c1 + alpha * alpha * c2
    beta = rho / c0
    cross = rest * curve + alpha * (c1 - c2)
    own = rest * rest * curve + 2.0 * rest * alpha * (c1 - c2) + alpha * alpha * (c2 - c3)
    alpha_next = rho / (own + 2.0 * beta * cross + beta * beta * curve)
    factor_z = jnp.broadcast_to(alpha + alpha_next * (rest + beta), (1, ny))
    factor_t = jnp.broadcast_to(alpha_next * alpha, (1, ny))

    for l, r in chunks:
        rows = slice(r, r + ROWS)
        mid = slice(PAD + r, PAD + r + ROWS)
        adj_ref[l, rows, :] = factor_z * z[l, mid, :] + factor_t * t[l, mid, :]
        for k, ref in enumerate((grad_x_ref, grad_y_ref, grad_v_ref)):
            ref[l, rows, :] = factor_z * ref[l, rows, :] + factor_t * of_t[k, l, rows, :]

    sent(*NAMES)
    each_peer(lambda peer: share(peer, me).wait_send())


def write_out(*refs):
    sem = refs[-1]
    copies = [pltpu.make_async_copy(refs[i], refs[4 + i], sem.at[i]) for i in range(4)]
    for copy in copies:
        copy.start()
    for copy in copies:
        copy.wait()


def body(sizes, *args):
    lay, nx, ny = args[0].shape
    group = sizes["gx"] * sizes["gy"] * sizes["gz"]
    block = jax.ShapeDtypeStruct((lay, nx, ny), F32)
    whole = pl.BlockSpec(memory_space=pltpu.HBM)
    scalars = pl.BlockSpec(memory_space=pltpu.SMEM)
    vmem = pl.BlockSpec(memory_space=pltpu.VMEM)
    flat = lambda dtype=F32: pltpu.VMEM((lay, nx, ny), dtype)
    tall = pltpu.VMEM((lay, nx + 2 * PAD, ny), F32)
    args = [pltpu.with_memory_space_constraint(a, pltpu.HBM) for a in args]
    results = pl.pallas_call(
        functools.partial(kernel, sizes, (lay, nx, ny)),
        out_shape=(block,) * 4,
        in_specs=[whole] * 5 + [scalars] * 2,
        out_specs=(vmem,) * 4,
        scratch_shapes=[
            flat(), tall, flat(jnp.int32), flat(jnp.int32), flat(),
            tall, flat(), flat(), flat(), tall, tall, pltpu.VMEM((3, lay, nx, ny), F32),
            pltpu.VMEM((3, lay, ny), F32), pltpu.VMEM((3, lay, ny), F32),
            pltpu.VMEM((5, 1, lay * nx), F32), pltpu.VMEM((5, 1, lay * nx), F32),
            pltpu.VMEM((5, nx, ny), F32),
            pltpu.VMEM((3 * lay, ny), F32), pltpu.VMEM((3 * lay, ny), F32),
            pltpu.VMEM((3, lay * nx), F32), pltpu.VMEM((3, lay * nx), F32),
            pltpu.VMEM((2, 1, ny), F32), pltpu.VMEM((2, 1, ny), F32),
            pltpu.VMEM((2, lay, LANES), F32), pltpu.VMEM((2, lay, LANES), F32),
            pltpu.VMEM((2, lay, lay * nx), F32), pltpu.VMEM((2, lay, lay * nx), F32),
            pltpu.VMEM((8, LANES), F32), pltpu.VMEM((group, 8, LANES), F32),
            pltpu.SemaphoreType.DMA((5,)),
            pltpu.SemaphoreType.DMA((len(NAMES),)), pltpu.SemaphoreType.DMA((len(NAMES),)),
            pltpu.SemaphoreType.DMA((group,)), pltpu.SemaphoreType.DMA((group,)),
        ],
        compiler_params=pltpu.CompilerParams(
            collective_id=0, has_side_effects=True, vmem_limit_bytes=32 * 1024 * 1024),
    )(*args)
    return pl.pallas_call(
        write_out,
        out_shape=(block,) * 4,
        in_specs=[pl.BlockSpec(memory_space=pl.ANY)] * 4, compiler_params=pltpu.CompilerParams(vmem_limit_bytes=1024*1024),
        out_specs=(whole,) * 4,
        scratch_shapes=[pltpu.SemaphoreType.DMA((4,))],
    )(*results)


def solution(mesh):
    placed = P(("parts", "gz"), "gx", "gy")
    sizes = {axis: mesh.shape[axis] for axis in ("gx", "gy", "gz")}
    return jax.shard_map(
        functools.partial(body, sizes),
        mesh=mesh,
        in_specs=(placed,) * 5 + (P(), P()),
        out_specs=(placed,) * 4,
        check_vma=False,
    )
```

```python
import functools

import jax
import jax.numpy as jnp
from jax import lax
from jax.experimental import pallas as pl
from jax.experimental.pallas import tpu as pltpu
from jax.sharding import PartitionSpec as P

F32 = jnp.float32
PAD = 8
ROWS = 16
LANES = 128
MESSAGES = {
    "cx": {"gx": 1}, "cy": {"gy": 1}, "cv": {"gz": 1},
    "vx": {"gx": -1}, "vy": {"gy": -1}, "vl": {"gz": -1},
    "zx_up": {"gx": 1}, "zy_up": {"gy": 1}, "zl_up": {"gz": 1}, "zl_dn": {"gz": -1},
    "xd": {"gx": -1}, "yd": {"gy": -1}, "tl": {"gz": -1},
    "lx_up": {"gx": -1, "gz": 1}, "lx_dn": {"gx": -1, "gz": -1},
    "ly_up": {"gy": -1, "gz": 1}, "ly_dn": {"gy": -1, "gz": -1},
    "ca": {"gx": -1, "gy": 1}, "cb": {"gx": -1, "gy": -1}, "cc": {"gx": -1, "gy": -1},
    "cd": {"gx": 1, "gy": -1},
}
NAMES = list(MESSAGES)


def kernel(
    sizes, dims,
    source_hbm, volt_hbm, class_x_hbm, class_y_hbm, via_hbm, sheet_ref, table_ref,
    adj_ref, grad_x_ref, grad_y_ref, grad_v_ref,
    source, volt, class_x, class_y, via, cond_x, cond_y, low_y, inverse, z, t, of_t,
    row_send, row_recv, col_send, col_recv, lay_recv,
    xd_send, xd_recv, yd_send, yd_recv, over_send, over_recv, row_end_send, row_end_recv,
    col_end_send, col_end_recv, part, parts,
    load_sem, send_sem, recv_sem, part_send, part_recv,
):
    lay, nx, ny = dims
    group = sizes["gx"] * sizes["gy"] * sizes["gz"]
    here = {axis: lax.axis_index(axis) for axis in ("gx", "gy", "gz")}
    me = (here["gx"] * sizes["gy"] + here["gy"]) * sizes["gz"] + here["gz"]
    inner = pl.ds(PAD, nx)
    first, last = PAD, PAD + nx - 1

    loads = []
    for i, (src, dst) in enumerate((
        (class_x_hbm, class_x), (class_y_hbm, class_y), (via_hbm, via),
        (source_hbm, source), (volt_hbm, volt.at[:, inner, :]),
    )):
        copy = pltpu.make_async_copy(src, dst, load_sem.at[i])
        copy.start()
        loads.append(copy)

    row_recv[...] = jnp.zeros_like(row_recv)
    col_recv[...] = jnp.zeros_like(col_recv)
    for ref in (xd_recv, yd_recv, over_recv, row_end_recv, col_end_recv):
        ref[...] = jnp.zeros_like(ref)
    z[:, PAD - 1, :] = jnp.zeros((lay, ny), F32)
    z[:, last + 1, :] = jnp.zeros((lay, ny), F32)

    empty = jnp.zeros((nx, ny), F32)

    @pl.when(here["gz"] == sizes["gz"] - 1)
    def _():
        for slot in (1, 3, 4):
            lay_recv[slot] = empty

    @pl.when(here["gz"] == 0)
    def _():
        for slot in (0, 2):
            lay_recv[slot] = empty

    def place(rank):
        gz = lax.rem(rank, sizes["gz"])
        rest = lax.div(rank, sizes["gz"])
        return {"gx": lax.div(rest, sizes["gy"]), "gy": lax.rem(rest, sizes["gy"]), "gz": gz}

    barrier = pltpu.get_barrier_semaphore()

    def each_peer(body):
        if group <= 32:
            for k in sorted(range(1, group), key=lambda k: -min(k, group - k)):
                body(lax.rem(me + k, group))
        else:
            lax.fori_loop(1, group, lambda k, c: (body(lax.rem(me + k, group)), c)[1], 0)

    each_peer(lambda peer: pl.semaphore_signal(
        barrier, inc=1, device_id=place(peer), device_id_type=pl.DeviceIdType.MESH))

    ROW = {"cx": 0, "vx": 1, "zx_up": 2}
    COL = {"cy": 0, "vy": 1, "zy_up": 2, "ly_up": 3, "ly_dn": 4}
    LAY = {"cv": 0, "vl": 1, "zl_up": 2, "zl_dn": 3, "tl": 4}
    LAY_SRC = {
        "cv": via.at[lay - 1], "vl": volt.at[0, inner, :], "zl_up": z.at[lay - 1, inner, :],
        "zl_dn": z.at[0, inner, :], "tl": t.at[0, inner, :],
    }

    OTHER = {
        "xd": (xd_send, xd_recv), "yd": (yd_send, yd_recv),
        "lx_up": (over_send.at[0], over_recv.at[0]), "lx_dn": (over_send.at[1], over_recv.at[1]),
        "ca": (row_end_send.at[0], row_end_recv.at[0]), "cb": (row_end_send.at[1], row_end_recv.at[1]),
        "cc": (col_end_send.at[0], col_end_recv.at[0]), "cd": (col_end_send.at[1], col_end_recv.at[1]),
    }

    def message(name):
        i = NAMES.index(name)
        if name in ROW:
            src, dst = row_send.at[ROW[name]], row_recv.at[ROW[name]]
        elif name in COL:
            src, dst = col_send.at[COL[name]], col_recv.at[COL[name]]
        elif name in OTHER:
            src, dst = OTHER[name]
        else:
            src, dst = LAY_SRC[name], lay_recv.at[LAY[name]]
        to = {axis: lax.rem(here[axis] + (way + sizes[axis]), sizes[axis])
              for axis, way in MESSAGES[name].items()}
        return pltpu.make_async_remote_copy(
            src_ref=src, dst_ref=dst, send_sem=send_sem.at[i], recv_sem=recv_sem.at[i],
            device_id=to, device_id_type=pl.DeviceIdType.MESH)

    def at_end(axis, way):
        return here[axis] == (sizes[axis] - 1 if way > 0 else 0)

    def guarded(name, sign, action):
        ways = MESSAGES[name]
        if any(sizes[axis] == 1 for axis in ways):
            return
        inside = [jnp.logical_not(at_end(axis, sign * way)) for axis, way in ways.items()]
        pl.when(functools.reduce(jnp.logical_and, inside))(action)

    def send(*names):
        for name in names:
            guarded(name, 1, message(name).start)

    def receive(*names):
        for name in names:
            guarded(name, -1, message(name).wait_recv)

    def sent(*names):
        for name in names:
            guarded(name, 1, message(name).wait_send)

    chunks = [(l, r) for l in range(lay) for r in range(0, nx, ROWS)]
    lane = lax.broadcasted_iota(jnp.int32, (ROWS, LANES), 1)

    def as_row(tile, at):
        return tile.reshape(lay * nx, LANES).T[at:at + 1, :]

    def put_col(name, tile, at):
        col_send[COL[name]] = as_row(tile, at)

    def as_col(row):
        return jnp.broadcast_to(row, (LANES, lay * nx)).T

    def col_halo(name):
        return as_col(col_recv[COL[name]])

    def from_left(value, edge):
        moved = pltpu.roll(value, 1, 1)
        head = jnp.where(lane == 0, edge, moved[:, :LANES])
        return jnp.concatenate([head, moved[:, LANES:]], axis=1)

    def from_right(value, edge):
        moved = pltpu.roll(value, ny - 1, 1)
        tail = jnp.where(lane == LANES - 1, edge, moved[:, ny - LANES:])
        return jnp.concatenate([moved[:, :ny - LANES], tail], axis=1)

    def edge_of(halo, l, r):
        return halo[l * nx + r:l * nx + r + ROWS]

    sheets = [sheet_ref[here["gz"] * lay + l] for l in range(lay)]
    classes = table_ref.shape[0]

    def look_up(label, l):
        value = jnp.full(label.shape, sheets[l] * table_ref[classes - 1], F32)
        for c in range(classes - 1):
            value = jnp.where(label == c, sheets[l] * table_ref[c], value)
        return value

    loads[0].wait()
    for l, r in chunks:
        cond_x[l, PAD + r:PAD + r + ROWS, :] = look_up(class_x[l, r:r + ROWS, :], l)

    @pl.when(at_end("gx", 1))
    def _():
        cond_x[:, last, :] = jnp.zeros((lay, ny), F32)

    loads[1].wait()
    for l, r in chunks:
        cond_y[l, r:r + ROWS, :] = look_up(class_y[l, r:r + ROWS, :], l)

    @pl.when(at_end("gy", 1))
    def _():
        for l in range(lay):
            tile = cond_y[l, :, ny - LANES:]
            spot = lax.broadcasted_iota(jnp.int32, tile.shape, 1)
            cond_y[l, :, ny - LANES:] = jnp.where(spot == LANES - 1, 0.0, tile)

    row_send[ROW["cx"]] = cond_x[:, last, :]
    put_col("cy", cond_y[:, :, ny - LANES:], LANES - 1)
    loads[2].wait()
    loads[3].wait()
    loads[4].wait()
    row_send[ROW["vx"]] = volt[:, first, :]
    put_col("vy", volt[:, inner, :LANES], 0)
    pl.semaphore_wait(barrier, group - 1)
    send("cv", "cx", "cy", "vx", "vy", "vl")
    receive("cx", "cy", "cv")

    cond_x[:, PAD - 1, :] = row_recv[ROW["cx"]]
    halo = col_halo("cy")
    moment0 = jnp.zeros((ROWS, ny), F32)
    for l, r in chunks:
        rows = slice(r, r + ROWS)
        cy = cond_y[l, rows, :]
        ly = from_left(cy, edge_of(halo, l, r))
        low_y[l, rows, :] = ly
        below = via[l - 1, rows, :] if l > 0 else lay_recv[LAY["cv"], rows, :]
        total = (cond_x[l, PAD + r:PAD + r + ROWS, :] + cond_x[l, PAD - 1 + r:PAD - 1 + r + ROWS, :]
                 + cy + ly + via[l, rows, :] + below)
        inv = 1.0 / total
        inverse[l, rows, :] = inv
        value = source[l, rows, :] * inv
        z[l, PAD + r:PAD + r + ROWS, :] = value
        moment0 = moment0 + source[l, rows, :] * value
    row_send[ROW["zx_up"]] = z[:, last, :]
    put_col("zy_up", z[:, inner, ny - LANES:], LANES - 1)
    send("zl_up", "zl_dn", "zx_up", "zy_up")

    one = lane[0:1]

    def from_left_row(value):
        moved = pltpu.roll(value, 1, 1)
        return jnp.concatenate([jnp.where(one == 0, 0.0, moved[:, :LANES]), moved[:, LANES:]], axis=1)

    def from_right_row(value):
        moved = pltpu.roll(value, ny - 1, 1)
        tail = jnp.where(one == LANES - 1, 0.0, moved[:, ny - LANES:])
        return jnp.concatenate([moved[:, :ny - LANES], tail], axis=1)

    col_parts = []
    for l in range(lay):
        row = z[l, first:first + 1, :]
        s = cond_x[l, first:first + 1, :] * z[l, first + 1:first + 2, :]
        s = s + cond_y[l, 0:1, :] * from_right_row(row) + low_y[l, 0:1, :] * from_left_row(row)
        tile = z[l, inner, :LANES]
        c = cond_x[l, inner, :LANES] * z[l, PAD + 1:PAD + 1 + nx, :LANES]
        c = c + cond_x[l, PAD - 1:PAD - 1 + nx, :LANES] * z[l, PAD - 1:PAD - 1 + nx, :LANES]
        c = c + cond_y[l, :, :LANES] * pltpu.roll(tile, LANES - 1, 1)
        if l + 1 < lay:
            s = s + via[l, 0:1, :] * z[l + 1, first:first + 1, :]
            c = c + via[l, :, :LANES] * z[l + 1, inner, :LANES]
        if l > 0:
            s = s + via[l - 1, 0:1, :] * z[l - 1, first:first + 1, :]
            c = c + via[l - 1, :, :LANES] * z[l - 1, inner, :LANES]
        xd_send[l:l + 1, :] = row
        xd_send[lay + l:lay + l + 1, :] = s
        xd_send[2 * lay + l:2 * lay + l + 1, :] = inverse[l, 0:1, :]
        col_parts.append(c)
    yd_send[0:1, :] = as_row(z[:, inner, :LANES], 0)
    yd_send[1:2, :] = as_row(jnp.stack(col_parts), 0)
    yd_send[2:3, :] = as_row(inverse[:, :, :LANES], 0)
    top = lay - 1
    over_send[0] = via[top, 0:1, :] * z[top, first:first + 1, :]
    over_send[1] = lay_recv[LAY["cv"], 0:1, :] * z[0, first:first + 1, :]
    blank = [jnp.zeros((nx, LANES), F32)] * (lay - 1)
    put_col("ly_up", jnp.stack([via[top, :, :LANES] * z[top, inner, :LANES]] + blank), 0)
    put_col("ly_dn", jnp.stack(blank + [lay_recv[LAY["cv"], :, :LANES] * z[0, inner, :LANES]]), 0)
    for l in range(lay):
        row = z[l, first:first + 1, :]
        tail = cond_y[l, 0:1, ny - LANES:] * row[:, ny - LANES:]
        row_end_send[0, l:l + 1, :] = jnp.where(one == 0, pltpu.roll(tail, 1, 1), 0.0)
        head = low_y[l, 0:1, :LANES] * row[:, :LANES]
        row_end_send[1, l:l + 1, :] = jnp.where(one == LANES - 1, pltpu.roll(head, LANES - 1, 1), 0.0)
        head = cond_x[l, PAD - 1:PAD, :LANES] * row[:, :LANES]
        col_end_send[0, l:l + 1, :] = jnp.broadcast_to(head[:, :1], (1, lay * nx))
        head = cond_x[l, last:last + 1, :LANES] * z[l, last:last + 1, :LANES]
        col_end_send[1, l:l + 1, :] = jnp.broadcast_to(head[:, :1], (1, lay * nx))
    send("xd", "yd", "lx_up", "lx_dn", "ly_up", "ly_dn", "ca", "cb", "cc", "cd")

    receive("vx", "vy", "vl")
    volt[:, last + 1, :] = row_recv[ROW["vx"]]
    halo = col_halo("vy")
    for l, r in chunks:
        rows = slice(r, r + ROWS)
        v = volt[l, PAD + r:PAD + r + ROWS, :]
        above = volt[l + 1, PAD + r:PAD + r + ROWS, :] if l + 1 < lay else lay_recv[LAY["vl"], rows, :]
        grad_x_ref[l, rows, :] = -sheets[l] * (v - volt[l, PAD + 1 + r:PAD + 1 + r + ROWS, :])
        grad_y_ref[l, rows, :] = -sheets[l] * (v - from_right(v, edge_of(halo, l, r)))
        grad_v_ref[l, rows, :] = above - v

    @pl.when(at_end("gx", 1))
    def _():
        grad_x_ref[:, nx - 1, :] = jnp.zeros((lay, ny), F32)

    @pl.when(at_end("gy", 1))
    def _():
        for l in range(lay):
            tile = grad_y_ref[l, :, ny - LANES:]
            spot = lax.broadcasted_iota(jnp.int32, tile.shape, 1)
            grad_y_ref[l, :, ny - LANES:] = jnp.where(spot == LANES - 1, 0.0, tile)

    receive("zx_up", "zy_up", "zl_up", "zl_dn", "xd", "yd")
    z[:, PAD - 1, :] = row_recv[ROW["zx_up"]]
    z[:, last + 1, :] = xd_recv[:lay, :]
    halo_lo = col_halo("zy_up")
    halo_hi = as_col(yd_recv[0:1, :])
    moment1 = jnp.zeros((ROWS, ny), F32)
    moment2 = jnp.zeros((ROWS, ny), F32)
    for l, r in chunks:
        rows = slice(r, r + ROWS)
        mid = slice(PAD + r, PAD + r + ROWS)
        lower = slice(PAD - 1 + r, PAD - 1 + r + ROWS)
        upper = slice(PAD + 1 + r, PAD + 1 + r + ROWS)
        here_z = z[l, mid, :]
        z_above = z[l + 1, mid, :] if l + 1 < lay else lay_recv[LAY["zl_dn"], rows, :]
        z_below = z[l - 1, mid, :] if l > 0 else lay_recv[LAY["zl_up"], rows, :]
        below = via[l - 1, rows, :] if l > 0 else lay_recv[LAY["cv"], rows, :]
        s = cond_x[l, mid, :] * z[l, upper, :] + cond_x[l, lower, :] * z[l, lower, :]
        s = s + cond_y[l, rows, :] * from_right(here_z, edge_of(halo_hi, l, r))
        s = s + low_y[l, rows, :] * from_left(here_z, edge_of(halo_lo, l, r))
        s = s + via[l, rows, :] * z_above + below * z_below
        value = s * inverse[l, rows, :]
        t[l, mid, :] = value
        moment1 = moment1 + here_z * s
        moment2 = moment2 + value * s
        if l == 0 and r + ROWS == nx:
            send("tl")

    receive("lx_up", "lx_dn", "ly_up", "ly_dn", "ca", "cb", "cc", "cd")
    for l in range(lay):
        s = xd_recv[lay + l:lay + l + 1, :] + cond_x[l, last:last + 1, :] * z[l, last:last + 1, :]
        if l == 0:
            s = s + over_recv[0]
        if l == lay - 1:
            s = s + over_recv[1]
        s = jnp.concatenate(
            [s[:, :LANES] + row_end_recv[0, l:l + 1, :], s[:, LANES:ny - LANES],
             s[:, ny - LANES:] + row_end_recv[1, l:l + 1, :]], axis=1)
        t[l, last + 1:last + 2, :] = s * xd_recv[2 * lay + l:2 * lay + l + 1, :]
    s = yd_recv[1:2, :] + col_send[COL["cy"]] * col_send[COL["zy_up"]]
    s = s + col_recv[COL["ly_up"]] + col_recv[COL["ly_dn"]]
    spot = lax.broadcasted_iota(jnp.int32, (1, lay * nx), 1)
    for l in range(lay):
        s = s + jnp.where(spot == l * nx + nx - 1, col_end_recv[0, l:l + 1, :], 0.0)
        s = s + jnp.where(spot == l * nx, col_end_recv[1, l:l + 1, :], 0.0)
    halo_t = as_col(s * yd_recv[2:3, :])
    moment3 = jnp.zeros((ROWS, ny), F32)
    for l, r in chunks:
        rows = slice(r, r + ROWS)
        mid = slice(PAD + r, PAD + r + ROWS)
        upper = slice(PAD + 1 + r, PAD + 1 + r + ROWS)
        here_t = t[l, mid, :]
        s = cond_x[l, mid, :] * t[l, upper, :]
        s = s + cond_y[l, rows, :] * from_right(here_t, edge_of(halo_t, l, r))
        if l + 1 < lay:
            s = s + via[l, rows, :] * t[l + 1, mid, :]
        moment3 = moment3 + here_t * s
    receive("tl")
    for r in range(0, nx, ROWS):
        rows = slice(r, r + ROWS)
        s = via[lay - 1, rows, :] * lay_recv[LAY["tl"], rows, :]
        moment3 = moment3 + t[lay - 1, PAD + r:PAD + r + ROWS, :] * s

    quarter = LANES // 4

    def fold(value):
        wide = sum(value[:, k:k + LANES] for k in range(0, ny, LANES))
        line = jnp.sum(wide, axis=0, keepdims=True)
        line = line + pltpu.roll(line, 2 * quarter, 1)
        return line + pltpu.roll(line, quarter, 1)

    packed = 2.0 * fold(moment3)
    for k, moment in ((2, moment2), (1, moment1), (0, moment0)):
        packed = jnp.where(one < (k + 1) * quarter, fold(moment), packed)
    part[...] = packed

    def share(peer, slot):
        return pltpu.make_async_remote_copy(
            src_ref=part, dst_ref=parts.at[slot], send_sem=part_send.at[peer], recv_sem=part_recv.at[slot],
            device_id=place(peer), device_id_type=pl.DeviceIdType.MESH)

    each_peer(lambda peer: share(peer, me).start())
    parts[me] = part[...]

    for l, r in chunks:
        rows = slice(r, r + ROWS)
        mid = slice(PAD + r, PAD + r + ROWS)
        upper = slice(PAD + 1 + r, PAD + 1 + r + ROWS)
        here_z, here_t = z[l, mid, :], t[l, mid, :]
        if l + 1 < lay:
            z_above, t_above = z[l + 1, mid, :], t[l + 1, mid, :]
        else:
            z_above, t_above = lay_recv[LAY["zl_dn"], rows, :], lay_recv[LAY["tl"], rows, :]
        volts = grad_x_ref[l, rows, :]
        grad_x_ref[l, rows, :] = volts * (here_z - z[l, upper, :])
        of_t[0, l, rows, :] = volts * (here_t - t[l, upper, :])
        volts = grad_y_ref[l, rows, :]
        grad_y_ref[l, rows, :] = volts * (here_z - from_right(here_z, edge_of(halo_hi, l, r)))
        of_t[1, l, rows, :] = volts * (here_t - from_right(here_t, edge_of(halo_t, l, r)))
        volts = grad_v_ref[l, rows, :]
        grad_v_ref[l, rows, :] = volts * (here_z - z_above)
        of_t[2, l, rows, :] = volts * (here_t - t_above)

    each_peer(lambda peer: share(peer, peer).wait_recv())
    summed = jnp.broadcast_to(jnp.sum(parts[...], axis=0), (8, LANES))
    spot = lax.broadcasted_iota(jnp.int32, (8, LANES), 1)
    low = lax.broadcasted_iota(jnp.int32, (8, LANES), 0) * quarter
    mine = jnp.logical_and(spot >= low, spot < low + quarter)
    totals = jnp.sum(jnp.where(mine, summed, 0.0), axis=1, keepdims=True)
    c0, c1, c2, c3 = (totals[k:k + 1, :] for k in range(4))
    curve = c0 - c1
    alpha = c0 / curve
    rest = -c1 / curve
    rho = rest * rest * c0 + 2.0 * rest * alpha * c1 + alpha * alpha * c2
    beta = rho / c0
    cross = rest * curve + alpha * (c1 - c2)
    own = rest * rest * curve + 2.0 * rest * alpha * (c1 - c2) + alpha * alpha * (c2 - c3)
    alpha_next = rho / (own + 2.0 * beta * cross + beta * beta * curve)
    factor_z = jnp.broadcast_to(alpha + alpha_next * (rest + beta), (1, ny))
    factor_t = jnp.broadcast_to(alpha_next * alpha, (1, ny))

    for l, r in chunks:
        rows = slice(r, r + ROWS)
        mid = slice(PAD + r, PAD + r + ROWS)
        adj_ref[l, rows, :] = factor_z * z[l, mid, :] + factor_t * t[l, mid, :]
        for k, ref in enumerate((grad_x_ref, grad_y_ref, grad_v_ref)):
            ref[l, rows, :] = factor_z * ref[l, rows, :] + factor_t * of_t[k, l, rows, :]

    sent(*NAMES)
    each_peer(lambda peer: share(peer, me).wait_send())


def write_out(*refs):
    sem = refs[-1]
    copies = [pltpu.make_async_copy(refs[i], refs[4 + i], sem.at[i]) for i in range(4)]
    for copy in copies:
        copy.start()
    for copy in copies:
        copy.wait()


def body(sizes, *args):
    lay, nx, ny = args[0].shape
    group = sizes["gx"] * sizes["gy"] * sizes["gz"]
    block = jax.ShapeDtypeStruct((lay, nx, ny), F32)
    whole = pl.BlockSpec(memory_space=pltpu.HBM)
    scalars = pl.BlockSpec(memory_space=pltpu.SMEM)
    vmem = pl.BlockSpec(memory_space=pltpu.VMEM)
    flat = lambda dtype=F32: pltpu.VMEM((lay, nx, ny), dtype)
    tall = pltpu.VMEM((lay, nx + 2 * PAD, ny), F32)
    args = [pltpu.with_memory_space_constraint(a, pltpu.HBM) for a in args]
    results = pl.pallas_call(
        functools.partial(kernel, sizes, (lay, nx, ny)),
        out_shape=(block,) * 4,
        in_specs=[whole] * 5 + [scalars] * 2,
        out_specs=(vmem,) * 4,
        scratch_shapes=[
            flat(), tall, flat(jnp.int32), flat(jnp.int32), flat(),
            tall, flat(), flat(), flat(), tall, tall, pltpu.VMEM((3, lay, nx, ny), F32),
            pltpu.VMEM((3, lay, ny), F32), pltpu.VMEM((3, lay, ny), F32),
            pltpu.VMEM((5, 1, lay * nx), F32), pltpu.VMEM((5, 1, lay * nx), F32),
            pltpu.VMEM((5, nx, ny), F32),
            pltpu.VMEM((3 * lay, ny), F32), pltpu.VMEM((3 * lay, ny), F32),
            pltpu.VMEM((3, lay * nx), F32), pltpu.VMEM((3, lay * nx), F32),
            pltpu.VMEM((2, 1, ny), F32), pltpu.VMEM((2, 1, ny), F32),
            pltpu.VMEM((2, lay, LANES), F32), pltpu.VMEM((2, lay, LANES), F32),
            pltpu.VMEM((2, lay, lay * nx), F32), pltpu.VMEM((2, lay, lay * nx), F32),
            pltpu.VMEM((1, LANES), F32), pltpu.VMEM((group, 1, LANES), F32),
            pltpu.SemaphoreType.DMA((5,)),
            pltpu.SemaphoreType.DMA((len(NAMES),)), pltpu.SemaphoreType.DMA((len(NAMES),)),
            pltpu.SemaphoreType.DMA((group,)), pltpu.SemaphoreType.DMA((group,)),
        ],
        compiler_params=pltpu.CompilerParams(
            collective_id=0, has_side_effects=True, vmem_limit_bytes=32 * 1024 * 1024),
    )(*args)
    return pl.pallas_call(
        write_out,
        out_shape=(block,) * 4,
        in_specs=[pl.BlockSpec(memory_space=pl.ANY)] * 4, compiler_params=pltpu.CompilerParams(vmem_limit_bytes=1024*1024),
        out_specs=(whole,) * 4,
        scratch_shapes=[pltpu.SemaphoreType.DMA((4,))],
    )(*results)


def solution(mesh):
    placed = P(("parts", "gz"), "gx", "gy")
    sizes = {axis: mesh.shape[axis] for axis in ("gx", "gy", "gz")}
    return jax.shard_map(
        functools.partial(body, sizes),
        mesh=mesh,
        in_specs=(placed,) * 5 + (P(), P()),
        out_specs=(placed,) * 4,
        check_vma=False,
    )
```

```python
import functools

import jax
import jax.numpy as jnp
from jax import lax
from jax.experimental import pallas as pl
from jax.experimental.pallas import tpu as pltpu
from jax.sharding import PartitionSpec as P

F32 = jnp.float32
PAD = 8
ROWS = 8
LANES = 128
MESSAGES = {
    "cx": {"gx": 1}, "cy": {"gy": 1}, "cv": {"gz": 1},
    "vx": {"gx": -1}, "vy": {"gy": -1}, "vl": {"gz": -1},
    "zx_up": {"gx": 1}, "zy_up": {"gy": 1}, "zl_up": {"gz": 1}, "zl_dn": {"gz": -1},
    "xd": {"gx": -1}, "yd": {"gy": -1}, "tl": {"gz": -1},
    "lx_up": {"gx": -1, "gz": 1}, "lx_dn": {"gx": -1, "gz": -1},
    "ly_up": {"gy": -1, "gz": 1}, "ly_dn": {"gy": -1, "gz": -1},
    "ca": {"gx": -1, "gy": 1}, "cb": {"gx": -1, "gy": -1}, "cc": {"gx": -1, "gy": -1},
    "cd": {"gx": 1, "gy": -1},
}
NAMES = list(MESSAGES)


def kernel(
    sizes, dims,
    source_hbm, volt_hbm, class_x_hbm, class_y_hbm, via_hbm, sheet_ref, table_ref,
    adj_ref, grad_x_ref, grad_y_ref, grad_v_ref,
    source, volt, class_x, class_y, via, cond_x, cond_y, low_y, inverse, z, t, of_t,
    row_send, row_recv, col_send, col_recv, lay_recv,
    xd_send, xd_recv, yd_send, yd_recv, over_send, over_recv, row_end_send, row_end_recv,
    col_end_send, col_end_recv, part, parts,
    load_sem, send_sem, recv_sem, part_send, part_recv,
):
    lay, nx, ny = dims
    group = sizes["gx"] * sizes["gy"] * sizes["gz"]
    here = {axis: lax.axis_index(axis) for axis in ("gx", "gy", "gz")}
    me = (here["gx"] * sizes["gy"] + here["gy"]) * sizes["gz"] + here["gz"]
    inner = pl.ds(PAD, nx)
    first, last = PAD, PAD + nx - 1

    loads = []
    for i, (src, dst) in enumerate((
        (class_x_hbm, class_x), (class_y_hbm, class_y), (via_hbm, via),
        (source_hbm, source), (volt_hbm, volt.at[:, inner, :]),
    )):
        copy = pltpu.make_async_copy(src, dst, load_sem.at[i])
        copy.start()
        loads.append(copy)

    row_recv[...] = jnp.zeros_like(row_recv)
    col_recv[...] = jnp.zeros_like(col_recv)
    for ref in (xd_recv, yd_recv, over_recv, row_end_recv, col_end_recv):
        ref[...] = jnp.zeros_like(ref)
    z[:, PAD - 1, :] = jnp.zeros((lay, ny), F32)
    z[:, last + 1, :] = jnp.zeros((lay, ny), F32)

    empty = jnp.zeros((nx, ny), F32)

    @pl.when(here["gz"] == sizes["gz"] - 1)
    def _():
        for slot in (1, 3, 4):
            lay_recv[slot] = empty

    @pl.when(here["gz"] == 0)
    def _():
        for slot in (0, 2):
            lay_recv[slot] = empty

    def place(rank):
        gz = lax.rem(rank, sizes["gz"])
        rest = lax.div(rank, sizes["gz"])
        return {"gx": lax.div(rest, sizes["gy"]), "gy": lax.rem(rest, sizes["gy"]), "gz": gz}

    barrier = pltpu.get_barrier_semaphore()

    def each_peer(body):
        if group <= 32:
            for k in sorted(range(1, group), key=lambda k: -min(k, group - k)):
                body(lax.rem(me + k, group))
        else:
            lax.fori_loop(1, group, lambda k, c: (body(lax.rem(me + k, group)), c)[1], 0)

    each_peer(lambda peer: pl.semaphore_signal(
        barrier, inc=1, device_id=place(peer), device_id_type=pl.DeviceIdType.MESH))

    ROW = {"cx": 0, "vx": 1, "zx_up": 2}
    COL = {"cy": 0, "vy": 1, "zy_up": 2, "ly_up": 3, "ly_dn": 4}
    LAY = {"cv": 0, "vl": 1, "zl_up": 2, "zl_dn": 3, "tl": 4}
    LAY_SRC = {
        "cv": via.at[lay - 1], "vl": volt.at[0, inner, :], "zl_up": z.at[lay - 1, inner, :],
        "zl_dn": z.at[0, inner, :], "tl": t.at[0, inner, :],
    }

    OTHER = {
        "xd": (xd_send, xd_recv), "yd": (yd_send, yd_recv),
        "lx_up": (over_send.at[0], over_recv.at[0]), "lx_dn": (over_send.at[1], over_recv.at[1]),
        "ca": (row_end_send.at[0], row_end_recv.at[0]), "cb": (row_end_send.at[1], row_end_recv.at[1]),
        "cc": (col_end_send.at[0], col_end_recv.at[0]), "cd": (col_end_send.at[1], col_end_recv.at[1]),
    }

    def message(name):
        i = NAMES.index(name)
        if name in ROW:
            src, dst = row_send.at[ROW[name]], row_recv.at[ROW[name]]
        elif name in COL:
            src, dst = col_send.at[COL[name]], col_recv.at[COL[name]]
        elif name in OTHER:
            src, dst = OTHER[name]
        else:
            src, dst = LAY_SRC[name], lay_recv.at[LAY[name]]
        to = {axis: lax.rem(here[axis] + (way + sizes[axis]), sizes[axis])
              for axis, way in MESSAGES[name].items()}
        return pltpu.make_async_remote_copy(
            src_ref=src, dst_ref=dst, send_sem=send_sem.at[i], recv_sem=recv_sem.at[i],
            device_id=to, device_id_type=pl.DeviceIdType.MESH)

    def at_end(axis, way):
        return here[axis] == (sizes[axis] - 1 if way > 0 else 0)

    def guarded(name, sign, action):
        ways = MESSAGES[name]
        if any(sizes[axis] == 1 for axis in ways):
            return
        inside = [jnp.logical_not(at_end(axis, sign * way)) for axis, way in ways.items()]
        pl.when(functools.reduce(jnp.logical_and, inside))(action)

    def send(*names):
        for name in names:
            guarded(name, 1, message(name).start)

    def receive(*names):
        for name in names:
            guarded(name, -1, message(name).wait_recv)

    def sent(*names):
        for name in names:
            guarded(name, 1, message(name).wait_send)

    chunks = [(l, r) for l in range(lay) for r in range(0, nx, ROWS)]
    lane = lax.broadcasted_iota(jnp.int32, (ROWS, LANES), 1)

    def as_row(tile, at):
        return tile.reshape(lay * nx, LANES).T[at:at + 1, :]

    def put_col(name, tile, at):
        col_send[COL[name]] = as_row(tile, at)

    def as_col(row):
        return jnp.broadcast_to(row, (LANES, lay * nx)).T

    def col_halo(name):
        return as_col(col_recv[COL[name]])

    def from_left(value, edge):
        moved = pltpu.roll(value, 1, 1)
        head = jnp.where(lane == 0, edge, moved[:, :LANES])
        return jnp.concatenate([head, moved[:, LANES:]], axis=1)

    def from_right(value, edge):
        moved = pltpu.roll(value, ny - 1, 1)
        tail = jnp.where(lane == LANES - 1, edge, moved[:, ny - LANES:])
        return jnp.concatenate([moved[:, :ny - LANES], tail], axis=1)

    def edge_of(halo, l, r):
        return halo[l * nx + r:l * nx + r + ROWS]

    sheets = [sheet_ref[here["gz"] * lay + l] for l in range(lay)]
    classes = table_ref.shape[0]

    def look_up(label, l):
        value = jnp.full(label.shape, sheets[l] * table_ref[classes - 1], F32)
        for c in range(classes - 1):
            value = jnp.where(label == c, sheets[l] * table_ref[c], value)
        return value

    loads[0].wait()
    for l, r in chunks:
        cond_x[l, PAD + r:PAD + r + ROWS, :] = look_up(class_x[l, r:r + ROWS, :], l)

    @pl.when(at_end("gx", 1))
    def _():
        cond_x[:, last, :] = jnp.zeros((lay, ny), F32)

    loads[1].wait()
    for l, r in chunks:
        cond_y[l, r:r + ROWS, :] = look_up(class_y[l, r:r + ROWS, :], l)

    @pl.when(at_end("gy", 1))
    def _():
        for l in range(lay):
            tile = cond_y[l, :, ny - LANES:]
            spot = lax.broadcasted_iota(jnp.int32, tile.shape, 1)
            cond_y[l, :, ny - LANES:] = jnp.where(spot == LANES - 1, 0.0, tile)

    row_send[ROW["cx"]] = cond_x[:, last, :]
    put_col("cy", cond_y[:, :, ny - LANES:], LANES - 1)
    loads[2].wait()
    loads[3].wait()
    loads[4].wait()
    row_send[ROW["vx"]] = volt[:, first, :]
    put_col("vy", volt[:, inner, :LANES], 0)
    pl.semaphore_wait(barrier, group - 1)
    send("cx", "cy", "cv", "vx", "vy", "vl")
    receive("cx", "cy", "cv")

    cond_x[:, PAD - 1, :] = row_recv[ROW["cx"]]
    halo = col_halo("cy")
    moment0 = jnp.zeros((ROWS, ny), F32)
    for l, r in chunks:
        rows = slice(r, r + ROWS)
        cy = cond_y[l, rows, :]
        ly = from_left(cy, edge_of(halo, l, r))
        low_y[l, rows, :] = ly
        below = via[l - 1, rows, :] if l > 0 else lay_recv[LAY["cv"], rows, :]
        total = (cond_x[l, PAD + r:PAD + r + ROWS, :] + cond_x[l, PAD - 1 + r:PAD - 1 + r + ROWS, :]
                 + cy + ly + via[l, rows, :] + below)
        inv = 1.0 / total
        inverse[l, rows, :] = inv
        value = source[l, rows, :] * inv
        z[l, PAD + r:PAD + r + ROWS, :] = value
        moment0 = moment0 + source[l, rows, :] * value
    row_send[ROW["zx_up"]] = z[:, last, :]
    put_col("zy_up", z[:, inner, ny - LANES:], LANES - 1)
    send("zl_up", "zl_dn", "zx_up", "zy_up")

    one = lane[0:1]

    def from_left_row(value):
        moved = pltpu.roll(value, 1, 1)
        return jnp.concatenate([jnp.where(one == 0, 0.0, moved[:, :LANES]), moved[:, LANES:]], axis=1)

    def from_right_row(value):
        moved = pltpu.roll(value, ny - 1, 1)
        tail = jnp.where(one == LANES - 1, 0.0, moved[:, ny - LANES:])
        return jnp.concatenate([moved[:, :ny - LANES], tail], axis=1)

    col_parts = []
    for l in range(lay):
        row = z[l, first:first + 1, :]
        s = cond_x[l, first:first + 1, :] * z[l, first + 1:first + 2, :]
        s = s + cond_y[l, 0:1, :] * from_right_row(row) + low_y[l, 0:1, :] * from_left_row(row)
        tile = z[l, inner, :LANES]
        c = cond_x[l, inner, :LANES] * z[l, PAD + 1:PAD + 1 + nx, :LANES]
        c = c + cond_x[l, PAD - 1:PAD - 1 + nx, :LANES] * z[l, PAD - 1:PAD - 1 + nx, :LANES]
        c = c + cond_y[l, :, :LANES] * pltpu.roll(tile, LANES - 1, 1)
        if l + 1 < lay:
            s = s + via[l, 0:1, :] * z[l + 1, first:first + 1, :]
            c = c + via[l, :, :LANES] * z[l + 1, inner, :LANES]
        if l > 0:
            s = s + via[l - 1, 0:1, :] * z[l - 1, first:first + 1, :]
            c = c + via[l - 1, :, :LANES] * z[l - 1, inner, :LANES]
        xd_send[l:l + 1, :] = row
        xd_send[lay + l:lay + l + 1, :] = s
        xd_send[2 * lay + l:2 * lay + l + 1, :] = inverse[l, 0:1, :]
        col_parts.append(c)
    yd_send[0:1, :] = as_row(z[:, inner, :LANES], 0)
    yd_send[1:2, :] = as_row(jnp.stack(col_parts), 0)
    yd_send[2:3, :] = as_row(inverse[:, :, :LANES], 0)
    top = lay - 1
    over_send[0] = via[top, 0:1, :] * z[top, first:first + 1, :]
    over_send[1] = lay_recv[LAY["cv"], 0:1, :] * z[0, first:first + 1, :]
    blank = [jnp.zeros((nx, LANES), F32)] * (lay - 1)
    put_col("ly_up", jnp.stack([via[top, :, :LANES] * z[top, inner, :LANES]] + blank), 0)
    put_col("ly_dn", jnp.stack(blank + [lay_recv[LAY["cv"], :, :LANES] * z[0, inner, :LANES]]), 0)
    for l in range(lay):
        row = z[l, first:first + 1, :]
        tail = cond_y[l, 0:1, ny - LANES:] * row[:, ny - LANES:]
        row_end_send[0, l:l + 1, :] = jnp.where(one == 0, pltpu.roll(tail, 1, 1), 0.0)
        head = low_y[l, 0:1, :LANES] * row[:, :LANES]
        row_end_send[1, l:l + 1, :] = jnp.where(one == LANES - 1, pltpu.roll(head, LANES - 1, 1), 0.0)
        head = cond_x[l, PAD - 1:PAD, :LANES] * row[:, :LANES]
        col_end_send[0, l:l + 1, :] = jnp.broadcast_to(head[:, :1], (1, lay * nx))
        head = cond_x[l, last:last + 1, :LANES] * z[l, last:last + 1, :LANES]
        col_end_send[1, l:l + 1, :] = jnp.broadcast_to(head[:, :1], (1, lay * nx))
    send("xd", "yd", "lx_up", "lx_dn", "ly_up", "ly_dn", "ca", "cb", "cc", "cd")

    receive("vx", "vy", "vl")
    volt[:, last + 1, :] = row_recv[ROW["vx"]]
    halo = col_halo("vy")
    for l, r in chunks:
        rows = slice(r, r + ROWS)
        v = volt[l, PAD + r:PAD + r + ROWS, :]
        above = volt[l + 1, PAD + r:PAD + r + ROWS, :] if l + 1 < lay else lay_recv[LAY["vl"], rows, :]
        grad_x_ref[l, rows, :] = -sheets[l] * (v - volt[l, PAD + 1 + r:PAD + 1 + r + ROWS, :])
        grad_y_ref[l, rows, :] = -sheets[l] * (v - from_right(v, edge_of(halo, l, r)))
        grad_v_ref[l, rows, :] = above - v

    @pl.when(at_end("gx", 1))
    def _():
        grad_x_ref[:, nx - 1, :] = jnp.zeros((lay, ny), F32)

    @pl.when(at_end("gy", 1))
    def _():
        for l in range(lay):
            tile = grad_y_ref[l, :, ny - LANES:]
            spot = lax.broadcasted_iota(jnp.int32, tile.shape, 1)
            grad_y_ref[l, :, ny - LANES:] = jnp.where(spot == LANES - 1, 0.0, tile)

    receive("zx_up", "zy_up", "zl_up", "zl_dn", "xd", "yd")
    z[:, PAD - 1, :] = row_recv[ROW["zx_up"]]
    z[:, last + 1, :] = xd_recv[:lay, :]
    halo_lo = col_halo("zy_up")
    halo_hi = as_col(yd_recv[0:1, :])
    moment1 = jnp.zeros((ROWS, ny), F32)
    moment2 = jnp.zeros((ROWS, ny), F32)
    for l, r in chunks:
        rows = slice(r, r + ROWS)
        mid = slice(PAD + r, PAD + r + ROWS)
        lower = slice(PAD - 1 + r, PAD - 1 + r + ROWS)
        upper = slice(PAD + 1 + r, PAD + 1 + r + ROWS)
        here_z = z[l, mid, :]
        z_above = z[l + 1, mid, :] if l + 1 < lay else lay_recv[LAY["zl_dn"], rows, :]
        z_below = z[l - 1, mid, :] if l > 0 else lay_recv[LAY["zl_up"], rows, :]
        below = via[l - 1, rows, :] if l > 0 else lay_recv[LAY["cv"], rows, :]
        s = cond_x[l, mid, :] * z[l, upper, :] + cond_x[l, lower, :] * z[l, lower, :]
        s = s + cond_y[l, rows, :] * from_right(here_z, edge_of(halo_hi, l, r))
        s = s + low_y[l, rows, :] * from_left(here_z, edge_of(halo_lo, l, r))
        s = s + via[l, rows, :] * z_above + below * z_below
        value = s * inverse[l, rows, :]
        t[l, mid, :] = value
        moment1 = moment1 + here_z * s
        moment2 = moment2 + value * s
        if l == 0 and r + ROWS == nx:
            send("tl")

    receive("lx_up", "lx_dn", "ly_up", "ly_dn", "ca", "cb", "cc", "cd")
    for l in range(lay):
        s = xd_recv[lay + l:lay + l + 1, :] + cond_x[l, last:last + 1, :] * z[l, last:last + 1, :]
        if l == 0:
            s = s + over_recv[0]
        if l == lay - 1:
            s = s + over_recv[1]
        s = jnp.concatenate(
            [s[:, :LANES] + row_end_recv[0, l:l + 1, :], s[:, LANES:ny - LANES],
             s[:, ny - LANES:] + row_end_recv[1, l:l + 1, :]], axis=1)
        t[l, last + 1:last + 2, :] = s * xd_recv[2 * lay + l:2 * lay + l + 1, :]
    s = yd_recv[1:2, :] + col_send[COL["cy"]] * col_send[COL["zy_up"]]
    s = s + col_recv[COL["ly_up"]] + col_recv[COL["ly_dn"]]
    spot = lax.broadcasted_iota(jnp.int32, (1, lay * nx), 1)
    for l in range(lay):
        s = s + jnp.where(spot == l * nx + nx - 1, col_end_recv[0, l:l + 1, :], 0.0)
        s = s + jnp.where(spot == l * nx, col_end_recv[1, l:l + 1, :], 0.0)
    halo_t = as_col(s * yd_recv[2:3, :])
    moment3 = jnp.zeros((ROWS, ny), F32)
    for l, r in chunks:
        rows = slice(r, r + ROWS)
        mid = slice(PAD + r, PAD + r + ROWS)
        upper = slice(PAD + 1 + r, PAD + 1 + r + ROWS)
        here_t = t[l, mid, :]
        s = cond_x[l, mid, :] * t[l, upper, :]
        s = s + cond_y[l, rows, :] * from_right(here_t, edge_of(halo_t, l, r))
        if l + 1 < lay:
            s = s + via[l, rows, :] * t[l + 1, mid, :]
        moment3 = moment3 + here_t * s
    receive("tl")
    for r in range(0, nx, ROWS):
        rows = slice(r, r + ROWS)
        s = via[lay - 1, rows, :] * lay_recv[LAY["tl"], rows, :]
        moment3 = moment3 + t[lay - 1, PAD + r:PAD + r + ROWS, :] * s

    quarter = LANES // 4

    def fold(value):
        wide = sum(value[:, k:k + LANES] for k in range(0, ny, LANES))
        line = jnp.sum(wide, axis=0, keepdims=True)
        line = line + pltpu.roll(line, 2 * quarter, 1)
        return line + pltpu.roll(line, quarter, 1)

    packed = 2.0 * fold(moment3)
    for k, moment in ((2, moment2), (1, moment1), (0, moment0)):
        packed = jnp.where(one < (k + 1) * quarter, fold(moment), packed)
    part[...] = packed

    def share(peer, slot):
        return pltpu.make_async_remote_copy(
            src_ref=part, dst_ref=parts.at[slot], send_sem=part_send.at[peer], recv_sem=part_recv.at[slot],
            device_id=place(peer), device_id_type=pl.DeviceIdType.MESH)

    each_peer(lambda peer: share(peer, me).start())
    parts[me] = part[...]

    for l, r in chunks:
        rows = slice(r, r + ROWS)
        mid = slice(PAD + r, PAD + r + ROWS)
        upper = slice(PAD + 1 + r, PAD + 1 + r + ROWS)
        here_z, here_t = z[l, mid, :], t[l, mid, :]
        if l + 1 < lay:
            z_above, t_above = z[l + 1, mid, :], t[l + 1, mid, :]
        else:
            z_above, t_above = lay_recv[LAY["zl_dn"], rows, :], lay_recv[LAY["tl"], rows, :]
        volts = grad_x_ref[l, rows, :]
        grad_x_ref[l, rows, :] = volts * (here_z - z[l, upper, :])
        of_t[0, l, rows, :] = volts * (here_t - t[l, upper, :])
        volts = grad_y_ref[l, rows, :]
        grad_y_ref[l, rows, :] = volts * (here_z - from_right(here_z, edge_of(halo_hi, l, r)))
        of_t[1, l, rows, :] = volts * (here_t - from_right(here_t, edge_of(halo_t, l, r)))
        volts = grad_v_ref[l, rows, :]
        grad_v_ref[l, rows, :] = volts * (here_z - z_above)
        of_t[2, l, rows, :] = volts * (here_t - t_above)

    each_peer(lambda peer: share(peer, peer).wait_recv())
    summed = jnp.broadcast_to(jnp.sum(parts[...], axis=0), (8, LANES))
    spot = lax.broadcasted_iota(jnp.int32, (8, LANES), 1)
    low = lax.broadcasted_iota(jnp.int32, (8, LANES), 0) * quarter
    mine = jnp.logical_and(spot >= low, spot < low + quarter)
    totals = jnp.sum(jnp.where(mine, summed, 0.0), axis=1, keepdims=True)
    c0, c1, c2, c3 = (totals[k:k + 1, :] for k in range(4))
    curve = c0 - c1
    alpha = c0 / curve
    rest = -c1 / curve
    rho = rest * rest * c0 + 2.0 * rest * alpha * c1 + alpha * alpha * c2
    beta = rho / c0
    cross = rest * curve + alpha * (c1 - c2)
    own = rest * rest * curve + 2.0 * rest * alpha * (c1 - c2) + alpha * alpha * (c2 - c3)
    alpha_next = rho / (own + 2.0 * beta * cross + beta * beta * curve)
    factor_z = jnp.broadcast_to(alpha + alpha_next * (rest + beta), (1, ny))
    factor_t = jnp.broadcast_to(alpha_next * alpha, (1, ny))

    for l, r in chunks:
        rows = slice(r, r + ROWS)
        mid = slice(PAD + r, PAD + r + ROWS)
        adj_ref[l, rows, :] = factor_z * z[l, mid, :] + factor_t * t[l, mid, :]
        for k, ref in enumerate((grad_x_ref, grad_y_ref, grad_v_ref)):
            ref[l, rows, :] = factor_z * ref[l, rows, :] + factor_t * of_t[k, l, rows, :]

    sent(*NAMES)
    each_peer(lambda peer: share(peer, me).wait_send())


def write_out(*refs):
    sem = refs[-1]
    copies = [pltpu.make_async_copy(refs[i], refs[4 + i], sem.at[i]) for i in range(4)]
    for copy in copies:
        copy.start()
    for copy in copies:
        copy.wait()


def body(sizes, *args):
    lay, nx, ny = args[0].shape
    group = sizes["gx"] * sizes["gy"] * sizes["gz"]
    block = jax.ShapeDtypeStruct((lay, nx, ny), F32)
    whole = pl.BlockSpec(memory_space=pltpu.HBM)
    scalars = pl.BlockSpec(memory_space=pltpu.SMEM)
    vmem = pl.BlockSpec(memory_space=pltpu.VMEM)
    flat = lambda dtype=F32: pltpu.VMEM((lay, nx, ny), dtype)
    tall = pltpu.VMEM((lay, nx + 2 * PAD, ny), F32)
    args = [pltpu.with_memory_space_constraint(a, pltpu.HBM) for a in args]
    results = pl.pallas_call(
        functools.partial(kernel, sizes, (lay, nx, ny)),
        out_shape=(block,) * 4,
        in_specs=[whole] * 5 + [scalars] * 2,
        out_specs=(vmem,) * 4,
        scratch_shapes=[
            flat(), tall, flat(jnp.int32), flat(jnp.int32), flat(),
            tall, flat(), flat(), flat(), tall, tall, pltpu.VMEM((3, lay, nx, ny), F32),
            pltpu.VMEM((3, lay, ny), F32), pltpu.VMEM((3, lay, ny), F32),
            pltpu.VMEM((5, 1, lay * nx), F32), pltpu.VMEM((5, 1, lay * nx), F32),
            pltpu.VMEM((5, nx, ny), F32),
            pltpu.VMEM((3 * lay, ny), F32), pltpu.VMEM((3 * lay, ny), F32),
            pltpu.VMEM((3, lay * nx), F32), pltpu.VMEM((3, lay * nx), F32),
            pltpu.VMEM((2, 1, ny), F32), pltpu.VMEM((2, 1, ny), F32),
            pltpu.VMEM((2, lay, LANES), F32), pltpu.VMEM((2, lay, LANES), F32),
            pltpu.VMEM((2, lay, lay * nx), F32), pltpu.VMEM((2, lay, lay * nx), F32),
            pltpu.VMEM((1, LANES), F32), pltpu.VMEM((group, 1, LANES), F32),
            pltpu.SemaphoreType.DMA((5,)),
            pltpu.SemaphoreType.DMA((len(NAMES),)), pltpu.SemaphoreType.DMA((len(NAMES),)),
            pltpu.SemaphoreType.DMA((group,)), pltpu.SemaphoreType.DMA((group,)),
        ],
        compiler_params=pltpu.CompilerParams(
            collective_id=0, has_side_effects=True, vmem_limit_bytes=32 * 1024 * 1024),
    )(*args)
    return pl.pallas_call(
        write_out,
        out_shape=(block,) * 4,
        in_specs=[pl.BlockSpec(memory_space=pl.ANY)] * 4, compiler_params=pltpu.CompilerParams(vmem_limit_bytes=1024*1024),
        out_specs=(whole,) * 4,
        scratch_shapes=[pltpu.SemaphoreType.DMA((4,))],
    )(*results)


def solution(mesh):
    placed = P(("parts", "gz"), "gx", "gy")
    sizes = {axis: mesh.shape[axis] for axis in ("gx", "gy", "gz")}
    return jax.shard_map(
        functools.partial(body, sizes),
        mesh=mesh,
        in_specs=(placed,) * 5 + (P(), P()),
        out_specs=(placed,) * 4,
        check_vma=False,
    )
```
